512 devices in a mesh: row: 32 (over z, y_lo), col: 16 (over x, y_hi, core).
Axes of the slice: x: 4, y: 8 (y_hi: 2, y_lo: 4; y = y_hi * 4 + y_lo), z: 8, core: 2. Of those that a mesh axis runs over, the one named last changes fastest.
Arguments:
- features: bfloat16 [131072, 128], P(('col', 'row')), may hold values from -6 to 6
- weight: bfloat16 [128, 256], replicated, may hold values from -0.5 to 0.5
- bias: float32 [256], replicated, may hold values from -3 to 3
- grad_out: bfloat16 [131072, 256], P(('row', 'col')), may hold values from -6 to 6
- tile_values: bfloat16 [32, 16, 128, 128, 128], P('row', 'col'), may hold values from -0.1875 to 0.1875
- tile_rows: int32 [32, 16, 128], P('row', 'col'), may hold values from 0 to 31
- tile_cols: int32 [32, 16, 128], P('row', 'col'), may hold values from 0 to 63
- tile_count: int32 [32, 16], P('row', 'col'), may hold values from 42 to 128, as said below
Outputs:
- hidden: bfloat16 [131072, 256], P(('row', 'col'))
- grad_weight: float32 [128, 256], replicated
- grad_bias: float32 [256], replicated
- grad_features: bfloat16 [131072, 128], P(('col', 'row'))
The draws below stay inside these ranges and needn't reach their ends.
Inputs may be any that keep to these rules, and one draw needn't show every extreme that they name: `tile_count`: slots below the count are live; some block has all 128 slots live.
All inputs are finite; a program needn't handle non-finite values.
Results may differ from the reference program's by a relative error of at most 0.03.
Values may be sent and summed in bfloat16 or wider, within the bound.
A program may use at most 64 MiB of HBM per device.

```python
import jax
import jax.numpy as jnp
from jax import lax

F_IN = 128
HID = 256
TILE = 128
NODE_DEV = 256
KT = 128
NODES = 131072
N_ROW = 32
N_COL = 16


def draw_tile_count(key, part):
    key = jax.random.fold_in(key, 11)
    first_key, second_key = jax.random.split(key)
    counts = jax.random.randint(first_key, (N_ROW * N_COL,), KT // 3, KT + 1)
    chosen = jax.random.randint(second_key, (), 0, N_ROW * N_COL)
    counts = counts.at[chosen].set(KT)
    return counts.reshape(N_ROW, N_COL).astype(jnp.int32)


def plant(drawn, key, smallest, high):
    shape = drawn.shape
    spot = [jax.random.randint(jax.random.fold_in(key, axis), (), 0, shape[axis]) for axis in range(len(shape))]
    drawn = drawn.at[tuple(spot)].set(smallest)
    longest = shape.index(max(shape))
    spot[longest] = (spot[longest] + 1) % shape[longest]
    return drawn.at[tuple(spot)].set(high)


def level_of(stream_key, shape, cuts, smallest, high):
    gain = 1.0
    for axis_at, blocks in cuts:
        draws = jax.random.uniform(jax.random.fold_in(jax.random.fold_in(stream_key, 6), axis_at), (blocks,), jnp.float32, smallest / len(cuts), high / len(cuts))
        gain = gain * jnp.repeat(jnp.exp(draws), shape[axis_at] // blocks).reshape((-1,) + (1,) * (len(shape) - 1 - axis_at))
    return gain


def gaussian(stream_key, shape, width, reach, shards=(), held_as=jnp.bfloat16):
    drawn = width * jax.random.normal(stream_key, shape, jnp.float32)
    if shards:
        drawn = drawn * level_of(stream_key, shape, shards, -0.22, 0.18)
    return jnp.clip(drawn, -reach, reach).astype(held_as)


def setup_inputs(seed: int = 0) -> dict:
    seeds = jax.random.split(jax.random.key(seed), 9)
    return {
        "features": gaussian(seeds[0], (NODES, F_IN), 1.0, 6.0, ((0, 512),)),
        "weight": gaussian(seeds[1], (F_IN, HID), F_IN ** -0.5, 0.5),
        "bias": gaussian(seeds[2], (HID,), 0.5, 3.0, (), jnp.float32),
        "grad_out": gaussian(seeds[3], (NODES, HID), 1.0, 6.0, ((0, 512),)),
        "tile_values": gaussian(seeds[4], (N_ROW, N_COL, KT, TILE, TILE), ((0.67 * KT * TILE * TILE / NODE_DEV) ** -0.5), 0.1875, ((0, 32), (1, 16))),
        "tile_rows": plant(jax.random.randint(seeds[5], (N_ROW, N_COL, KT), 0, NODE_DEV * N_COL // TILE), jax.random.fold_in(seeds[5], 1), 0, (NODE_DEV * N_COL // TILE) - 1).astype(jnp.int32),
        "tile_cols": plant(jax.random.randint(seeds[6], (N_ROW, N_COL, KT), 0, NODE_DEV * N_ROW // TILE), jax.random.fold_in(seeds[6], 1), 0, (NODE_DEV * N_ROW // TILE) - 1).astype(jnp.int32),
        "tile_count": draw_tile_count(jax.random.fold_in(seeds[8], 71), 0),
    }


def rounded(values):
    return lax.optimization_barrier(values.astype(jnp.bfloat16)).astype(jnp.float32)


def reference(features, weight, bias, grad_out, tile_values, tile_rows, tile_cols, tile_count):
    row_tiles = NODE_DEV * N_COL // TILE
    col_tiles = NODE_DEV * N_ROW // TILE
    blocks = N_ROW * N_COL
    flat_values = tile_values.reshape(blocks, KT, TILE, TILE)
    flat_rows = tile_rows.reshape(blocks, KT)
    flat_cols = tile_cols.reshape(blocks, KT)
    flat_count = tile_count.reshape(blocks)
    slot_ids = jnp.arange(KT, dtype=jnp.int32)
    feature_tiles = features.reshape(N_COL * col_tiles, TILE, F_IN)

    def forward_step(carry, block_id):
        r_index = (block_id // N_COL).astype(jnp.int32)
        c_index = (block_id % N_COL).astype(jnp.int32)
        live = (slot_ids < flat_count[block_id]).astype(jnp.float32)
        values = flat_values[block_id].astype(jnp.float32) * live[:, None, None]
        picked = feature_tiles[c_index * col_tiles + flat_cols[block_id]].astype(jnp.float32)
        products = jnp.einsum("kij,kjf->kif", values, picked)
        summed = jax.ops.segment_sum(products, flat_rows[block_id], num_segments=row_tiles)
        start = (r_index * row_tiles).astype(jnp.int32)
        current = lax.dynamic_slice_in_dim(carry, start, row_tiles, 0)
        carry = lax.dynamic_update_slice_in_dim(carry, current + rounded(summed), start, 0)
        return carry, None

    init = jnp.zeros((N_ROW * row_tiles, TILE, F_IN), jnp.float32)
    summed_all, _ = lax.scan(forward_step, init, jnp.arange(blocks, dtype=jnp.int32))
    aggregate = summed_all.reshape(NODES, F_IN).astype(jnp.bfloat16)
    preact = jnp.dot(aggregate, weight, preferred_element_type=jnp.float32) + bias
    sigmoid_pre = jax.nn.sigmoid(preact)
    hidden = (preact * sigmoid_pre).astype(jnp.bfloat16)
    slope_factor = sigmoid_pre * (1.0 + preact * (1.0 - sigmoid_pre))
    grad_pre = (grad_out.astype(jnp.float32) * slope_factor).astype(jnp.bfloat16)
    grad_weight = jnp.dot(aggregate.T, grad_pre, preferred_element_type=jnp.float32)
    grad_bias = jnp.sum(grad_pre.astype(jnp.float32), axis=0)
    grad_aggregate = jnp.dot(grad_pre, weight.T, preferred_element_type=jnp.float32).astype(jnp.bfloat16)
    grad_tiles = grad_aggregate.reshape(N_ROW * row_tiles, TILE, F_IN)

    def backward_step(carry, block_id):
        r_index = (block_id // N_COL).astype(jnp.int32)
        c_index = (block_id % N_COL).astype(jnp.int32)
        live = (slot_ids < flat_count[block_id]).astype(jnp.float32)
        values = flat_values[block_id].astype(jnp.float32) * live[:, None, None]
        picked = grad_tiles[r_index * row_tiles + flat_rows[block_id]].astype(jnp.float32)
        products = jnp.einsum("kji,kjf->kif", values, picked)
        summed = jax.ops.segment_sum(products, flat_cols[block_id], num_segments=col_tiles)
        start = (c_index * col_tiles).astype(jnp.int32)
        current = lax.dynamic_slice_in_dim(carry, start, col_tiles, 0)
        carry = lax.dynamic_update_slice_in_dim(carry, current + rounded(summed), start, 0)
        return carry, None

    init_back = jnp.zeros((N_COL * col_tiles, TILE, F_IN), jnp.float32)
    back_all, _ = lax.scan(backward_step, init_back, jnp.arange(blocks, dtype=jnp.int32))
    grad_features = back_all.reshape(NODES, F_IN).astype(jnp.bfloat16)
    return hidden, grad_weight, grad_bias, grad_features
```

```python
import functools

import jax
import jax.numpy as jnp
from jax import lax
from jax.experimental import pallas as pl
from jax.experimental.pallas import tpu as pltpu
from jax.sharding import PartitionSpec as P

MESH = pl.DeviceIdType.MESH
F32 = jnp.float32
BF16 = jnp.bfloat16

Z, YL, X, YH, CORE = 8, 4, 4, 2, 2
ROWS, COLS = Z * YL, X * YH * CORE
TILE = 128
NODE = 256
WIDTH = 128
HID = 256
SLOTS = 128
ROW_TILES = COLS * NODE // TILE
COL_TILES = ROWS * NODE // TILE
SPLIT = 192
REST = NODE - SPLIT
VMEM_LIMIT = 56 * 1024 * 1024


def row_of(z, y):
    return z * YL + y


def col_of(x, yh, core):
    return (x * YH + yh) * CORE + core


def where_am_i():
    row = lax.axis_index("row")
    col = lax.axis_index("col")
    return row, col, row // YL, row % YL, col // (YH * CORE), (col // CORE) % YH, col % CORE


def greet(peers):
    barrier = pltpu.get_barrier_semaphore()
    for peer in peers:
        pl.semaphore_signal(barrier, inc=1, device_id=peer, device_id_type=MESH)
    pl.semaphore_wait(barrier, len(peers))


class Sender:
    def __init__(self, sems):
        self.sems = sems
        self.started = []

    def send(self, src, dst, recv_sem, peer):
        copy = pltpu.make_async_remote_copy(
            src_ref=src,
            dst_ref=dst,
            send_sem=self.sems.at[len(self.started)],
            recv_sem=recv_sem,
            device_id=peer,
            device_id_type=MESH,
        )
        copy.start()
        self.started.append(copy)

    def finish(self):
        for copy in self.started:
            copy.wait_send()


def arrived(dst, recv_sem, peer):
    pltpu.make_async_remote_copy(
        src_ref=dst, dst_ref=dst, send_sem=recv_sem, recv_sem=recv_sem, device_id=peer, device_id_type=MESH
    ).wait_recv()


GATHER_SENDS = 3 + 28 + 7 + 24


def gather_row_kernel(feat, panel, sends, recv_a, recv_b):
    row, col, z, y, _, _, _ = where_am_i()
    up = (row_of((z + 1) % Z, y), col)
    down = (row_of((z + Z - 1) % Z, y), col)
    near = [(row_of(z, (y + j) % YL), col) for j in range(1, YL)]
    greet([up, down] + near)
    out = Sender(sends)
    part_a, part_b = pl.ds(0, SPLIT), pl.ds(SPLIT, REST)

    def shard(dz, j):
        return row_of((z + Z + dz) % Z, (y + j) % YL)

    def a(s):
        return panel.at[s, part_a], recv_a.at[s]

    def b(s):
        return panel.at[s, part_b], recv_b.at[s]

    def pass_on(src, s, way, peer):
        dst, sem = way(s)
        out.send(src, dst, sem, peer)

    mine = feat.at[part_a], feat.at[part_b]
    pass_on(mine[1], row, b, up)
    pass_on(mine[1], row, b, down)
    for j in range(1, YL):
        pass_on(mine[0], row, a, near[j - 1])
    pass_on(mine[0], row, a, up)
    pass_on(mine[0], row, a, down)
    for j in range(1, YL):
        pass_on(mine[1], row, b, near[j - 1])
    panel[row] = feat[...]
    for j in range(1, YL):
        s = shard(0, j)
        arrived(*a(s), near[j - 1])
        pass_on(a(s)[0], s, a, up)
        pass_on(a(s)[0], s, a, down)
    for d in range(1, Z // 2):
        for sign, source, target in ((-1, down, up), (1, up, down)):
            s = shard(sign * d, 0)
            arrived(*b(s), source)
            if d < Z // 2 - 1 or sign < 0:
                pass_on(b(s)[0], s, b, target)
            for j in range(1, YL):
                pass_on(b(s)[0], s, b, near[j - 1])
        for j in range(YL):
            for sign, source, target in ((-1, down, up), (1, up, down)):
                s = shard(sign * d, j)
                arrived(*a(s), source)
                if d < Z // 2 - 1 or (j < 2) == (sign < 0):
                    pass_on(a(s)[0], s, a, target)
    s = shard(Z // 2, 0)
    arrived(*b(s), down)
    for j in range(1, YL):
        pass_on(b(s)[0], s, b, near[j - 1])
    for j in range(YL):
        arrived(*a(shard(Z // 2, j)), down if j < 2 else up)
    for dz in range(Z):
        for j in range(1, YL):
            arrived(*b(shard(dz, j)), near[j - 1])
    out.finish()


def gather_row(features):
    return pl.pallas_call(
        gather_row_kernel,
        out_shape=jax.ShapeDtypeStruct((ROWS, NODE, WIDTH), BF16),
        in_specs=[pl.BlockSpec(memory_space=pltpu.VMEM)],
        out_specs=pl.BlockSpec(memory_space=pltpu.VMEM),
        scratch_shapes=[
            pltpu.SemaphoreType.DMA((GATHER_SENDS,)),
            pltpu.SemaphoreType.DMA((ROWS,)),
            pltpu.SemaphoreType.DMA((ROWS,)),
        ],
        compiler_params=pltpu.CompilerParams(
            collective_id=0, has_side_effects=True, vmem_limit_bytes=VMEM_LIMIT
        ),
    )(features)


STEP = 16
UNROLL = 8


def tiles_kernel(transposed, n_out, pick, place, count, values, panel, out, total):
    step = pl.program_id(0)

    @pl.when(step == 0)
    def _():
        total[...] = jnp.zeros_like(total)

    live = count[0]

    @pl.when(step * STEP < live)
    def _():
        def group(g, carry):
            for u in range(UNROLL):
                k = g * UNROLL + u
                slot = step * STEP + k
                here = panel[pick[slot]]
                dims = (((0,), (0,)), ((), ())) if transposed else (((1,), (0,)), ((), ()))
                product = lax.dot_general(values[k], here, dims, preferred_element_type=F32)
                at = jnp.where(slot < live, place[slot], n_out)
                total[at] += product
            return carry

        lax.fori_loop(0, STEP // UNROLL, group, 0)

    @pl.when(step == SLOTS // STEP - 1)
    def _():
        out[...] = total[:n_out].astype(BF16)


def tile_products(values, pick, place, count, panel, n_out, transposed):
    n_in = panel.shape[0]
    return pl.pallas_call(
        functools.partial(tiles_kernel, transposed, n_out),
        out_shape=jax.ShapeDtypeStruct((n_out, TILE, WIDTH), BF16),
        grid_spec=pltpu.PrefetchScalarGridSpec(
            num_scalar_prefetch=3,
            grid=(SLOTS // STEP,),
            in_specs=[
                pl.BlockSpec((STEP, TILE, TILE), lambda i, *_: (i, 0, 0)),
                pl.BlockSpec((n_in, TILE, WIDTH), lambda i, *_: (0, 0, 0)),
            ],
            out_specs=pl.BlockSpec((n_out, TILE, WIDTH), lambda i, *_: (0, 0, 0)),
            scratch_shapes=[pltpu.VMEM((n_out + 1, TILE, WIDTH), F32)],
        ),
        compiler_params=pltpu.CompilerParams(
            dimension_semantics=("arbitrary",), vmem_limit_bytes=VMEM_LIMIT
        ),
    )(pick, place, count, values, panel)


MIDDLE_SENDS = 4 + 3 + 1 + 1 + 6 + 8


def middle_kernel(
    partial, grad_out, weight, bias, hidden, block, gw, gb,
    paired, pair_in, x_in, y_out, y_in, sends, pair_sem, x_sem, y_sem, gather_sem,
):
    row, col, _, _, x, yh, core = where_am_i()
    sibling = (row, col_of(x, yh, 1 - core))
    far = (row, col_of(x, 1 - yh, core))
    ring = [(row, col_of((x + d) % X, yh, core)) for d in range(1, X)]
    greet([sibling, far] + ring)
    out = Sender(sends)
    order = [2, 1, 3, 0]
    for d in order:
        other = (x + d) % X
        out.send(partial.at[other, :, 1 - core], pair_in.at[d], pair_sem.at[d], sibling)
    for d in order:
        other = (x + d) % X
        arrived(pair_in.at[d], pair_sem.at[d], sibling)
        for h in range(YH):
            paired[d, h] = (partial[other, h, core].astype(F32) + pair_in[d, h].astype(F32)).astype(BF16)
        if d:
            out.send(paired.at[d], x_in.at[X - d], x_sem.at[X - d], ring[d - 1])
    for d in range(1, X):
        arrived(x_in.at[d], x_sem.at[d], ring[d - 1])

    def summed(h):
        acc = paired[0, h].astype(F32)
        for d in range(1, X):
            acc += x_in[d, h].astype(F32)
        return acc

    y_out[...] = summed(1 - yh).astype(BF16)
    out.send(y_out, y_in, y_sem.at[0], far)
    own = summed(yh)
    arrived(y_in, y_sem.at[0], far)
    aggregate = (own + y_in[...].astype(F32)).astype(BF16)
    preact = jnp.dot(aggregate, weight[...], preferred_element_type=F32) + bias[...]
    sigmoid = jax.nn.sigmoid(preact)
    slope = sigmoid * (1.0 + preact * (1.0 - sigmoid))
    grad_pre = (grad_out[...].astype(F32) * slope).astype(BF16)
    block[col] = lax.dot_general(
        grad_pre, weight[...], (((1,), (1,)), ((), ())), preferred_element_type=F32
    ).astype(BF16)

    def g(c):
        return block.at[c], gather_sem.at[c]

    def pass_on(c, peer):
        out.send(block.at[c], block.at[c], gather_sem.at[c], peer)

    pass_on(col, far)
    for d in order[:3]:
        pass_on(col, ring[d - 1])
    pass_on(col, sibling)
    hidden[...] = (preact * sigmoid).astype(BF16)
    gw[...] = lax.dot_general(aggregate, grad_pre, (((0,), (0,)), ((), ())), preferred_element_type=F32)
    gb[...] = jnp.broadcast_to(jnp.sum(grad_pre.astype(F32), axis=0, keepdims=True), gb.shape)
    c = col_of(x, 1 - yh, core)
    arrived(*g(c), far)
    for d in order[:3]:
        pass_on(c, ring[d - 1])
    pass_on(c, sibling)
    for d in (1, 3, 2):
        for h in (yh, 1 - yh):
            c = col_of((x + d) % X, h, core)
            arrived(*g(c), ring[d - 1])
            pass_on(c, sibling)
    for d in range(X):
        for h in range(YH):
            arrived(*g(col_of((x + d) % X, h, 1 - core)), sibling)
    out.finish()


def middle(partial, grad_out, weight, bias):
    return pl.pallas_call(
        middle_kernel,
        out_shape=(
            jax.ShapeDtypeStruct((NODE, HID), BF16),
            jax.ShapeDtypeStruct((COLS, NODE, WIDTH), BF16),
            jax.ShapeDtypeStruct((WIDTH, HID), F32),
            jax.ShapeDtypeStruct((8, HID), F32),
        ),
        in_specs=[pl.BlockSpec(memory_space=pltpu.VMEM)] * 4,
        out_specs=(pl.BlockSpec(memory_space=pltpu.VMEM),) * 4,
        scratch_shapes=[
            pltpu.VMEM((X, YH, NODE, WIDTH), BF16),
            pltpu.VMEM((X, YH, NODE, WIDTH), BF16),
            pltpu.VMEM((X, YH, NODE, WIDTH), BF16),
            pltpu.VMEM((NODE, WIDTH), BF16),
            pltpu.VMEM((NODE, WIDTH), BF16),
            pltpu.SemaphoreType.DMA((MIDDLE_SENDS,)),
            pltpu.SemaphoreType.DMA((X,)),
            pltpu.SemaphoreType.DMA((X,)),
            pltpu.SemaphoreType.DMA((1,)),
            pltpu.SemaphoreType.DMA((COLS,)),
        ],
        compiler_params=pltpu.CompilerParams(
            collective_id=1, has_side_effects=True, vmem_limit_bytes=VMEM_LIMIT
        ),
    )(partial, grad_out, weight, bias)


PIECE = WIDTH // COLS
SCATTER_SENDS = 3 + 7 + 28 + 3 + (COLS - 1) * 2 + 3 + 7


def scatter_row_kernel(
    partial, gw, gb, result, gw_out, gb_out,
    a_out, a_in, near_out, near_in, b_first, b_sum, b_out, b_in,
    piece, piece_in, near_piece, far_piece, near_piece_in, far_piece_in,
    sends, a_sem, near_sem, b_first_sem, b_sem, piece_sem, np_sem, fp_sem, last_sem,
):
    row, col, z, y, _, _, _ = where_am_i()
    up = (row_of((z + 1) % Z, y), col)
    down = (row_of((z + Z - 1) % Z, y), col)
    near = [(row_of(z, (y + j) % YL), col) for j in range(1, YL)]
    along = [(row_of((z + d) % Z, y), col) for d in range(1, Z)]
    across = [(row, (col + d) % COLS) for d in range(1, COLS)]
    greet(near + along + across)
    out = Sender(sends)
    part_a, part_b = pl.ds(0, SPLIT), pl.ds(SPLIT, REST)
    half = Z // 2
    ways = ((0, 1, up, down), (1, -1, down, up))

    def own_a(dz, j):
        return partial.at[(z + Z + dz) % Z, (y + j) % YL, part_a]

    for j in range(1, YL):
        out.send(partial.at[:, (y + j) % YL, part_b], b_first.at[YL - j], b_first_sem.at[YL - j], near[j - 1])
    for j in (1, 2, 3, 0):
        way, sign, target, _ = ways[0] if j < 2 else ways[1]
        out.send(own_a(half, j), a_in.at[way, 0, j], a_sem.at[way, 0, j], target)
    for j in (1, 2, 3, 0):
        way, sign, target, _ = ways[1] if j < 2 else ways[0]
        out.send(own_a(sign * (half - 1), j), a_in.at[way, 1, j], a_sem.at[way, 1, j], target)

    for p in range(COLS):
        piece[p, 0:PIECE] = gw[p * PIECE:(p + 1) * PIECE]
        piece[p, PIECE:] = gb[...]
    for d in range(1, COLS):
        to = (col + d) % COLS
        out.send(piece.at[to], piece_in.at[COLS - d], piece_sem.at[COLS - d], across[d - 1])

    for j in (1, 2, 3, 0):
        way, sign, target, source = ways[0] if j < 2 else ways[1]
        arrived(a_in.at[way, 0, j], a_sem.at[way, 0, j], source)
        a_out[way, 1, j] = (own_a(sign * (half - 1), j)[...].astype(F32) + a_in[way, 0, j].astype(F32)).astype(BF16)
        out.send(a_out.at[way, 1, j], a_in.at[way, 1, j], a_sem.at[way, 1, j], target)

    for j in range(1, YL):
        arrived(b_first.at[j], b_first_sem.at[j], near[j - 1])
    for dz in range(Z):
        at = (z + dz) % Z
        acc = partial[at, y, SPLIT:].astype(F32)
        for j in range(1, YL):
            acc += b_first[j, at].astype(F32)
        b_sum[dz] = acc

    def rest_step(step):
        for way, sign, target, source in ways:
            if step == 0 and way == 1:
                continue
            acc = b_sum[(sign * (half - step)) % Z]
            if step > (0 if way == 0 else 1):
                arrived(b_in.at[way, step - 1], b_sem.at[way, step - 1], source)
                acc = acc + b_in[way, step - 1].astype(F32)
            b_out[way, step] = acc.astype(BF16)
            out.send(b_out.at[way, step], b_in.at[way, step], b_sem.at[way, step], target)

    rest_step(0)
    for step in (2, 3):
        for j in (1, 2, 3, 0):
            for way, sign, target, source in ways:
                arrived(a_in.at[way, step - 1, j], a_sem.at[way, step - 1, j], source)
                a_out[way, step, j] = (
                    own_a(sign * (half - step), j)[...].astype(F32) + a_in[way, step - 1, j].astype(F32)
                ).astype(BF16)
                out.send(a_out.at[way, step, j], a_in.at[way, step, j], a_sem.at[way, step, j], target)
        rest_step(step - 1)
        if step == 2:
            acc = piece[col]
            for d in range(1, COLS):
                arrived(piece_in.at[d], piece_sem.at[d], across[d - 1])
                acc = acc + piece_in[d]
            near_piece[...] = acc
            for j in range(1, YL):
                out.send(near_piece, near_piece_in.at[YL - j], np_sem.at[YL - j], near[j - 1])
        else:
            acc = near_piece[...]
            for j in range(1, YL):
                arrived(near_piece_in.at[j], np_sem.at[j], near[j - 1])
                acc = acc + near_piece_in[j]
            far_piece[...] = acc
            for d in range(1, Z):
                out.send(far_piece, far_piece_in.at[Z - d], fp_sem.at[Z - d], along[d - 1])
    rest_step(3)

    def final_a(j):
        acc = own_a(0, j)[...].astype(F32)
        for way, _, _, source in ways:
            arrived(a_in.at[way, 3, j], a_sem.at[way, 3, j], source)
            acc += a_in[way, 3, j].astype(F32)
        return acc

    for j in range(1, YL):
        near_out[j] = final_a(j).astype(BF16)
        out.send(near_out.at[j], near_in.at[YL - j], near_sem.at[YL - j], near[j - 1])
    mine = final_a(0)

    acc = far_piece[...]
    for d in range(1, Z):
        arrived(far_piece_in.at[d], fp_sem.at[d], along[d - 1])
        acc = acc + far_piece_in[d]
    gw_out[col] = acc[0:PIECE]
    gb_out[...] = acc[PIECE:]
    for d in range(1, COLS):
        out.send(gw_out.at[col], gw_out.at[col], last_sem.at[col], across[d - 1])

    acc = b_sum[0]
    for way, _, _, source in ways:
        arrived(b_in.at[way, 3], b_sem.at[way, 3], source)
        acc = acc + b_in[way, 3].astype(F32)
    result[SPLIT:] = acc.astype(BF16)
    for j in range(1, YL):
        arrived(near_in.at[j], near_sem.at[j], near[j - 1])
        mine += near_in[j].astype(F32)
    result[:SPLIT] = mine.astype(BF16)
    for d in range(1, COLS):
        at = (col + d) % COLS
        arrived(gw_out.at[at], last_sem.at[at], across[d - 1])
    out.finish()


def scatter_row(partial, gw, gb):
    return pl.pallas_call(
        scatter_row_kernel,
        out_shape=(
            jax.ShapeDtypeStruct((NODE, WIDTH), BF16),
            jax.ShapeDtypeStruct((COLS, PIECE, HID), F32),
            jax.ShapeDtypeStruct((8, HID), F32),
        ),
        in_specs=[pl.BlockSpec(memory_space=pltpu.VMEM)] * 3,
        out_specs=(pl.BlockSpec(memory_space=pltpu.VMEM),) * 3,
        scratch_shapes=[
            pltpu.VMEM((2, 4, YL, SPLIT, WIDTH), BF16),
            pltpu.VMEM((2, 4, YL, SPLIT, WIDTH), BF16),
            pltpu.VMEM((YL, SPLIT, WIDTH), BF16),
            pltpu.VMEM((YL, SPLIT, WIDTH), BF16),
            pltpu.VMEM((YL, Z, REST, WIDTH), BF16),
            pltpu.VMEM((Z, REST, WIDTH), F32),
            pltpu.VMEM((2, 4, REST, WIDTH), BF16),
            pltpu.VMEM((2, 4, REST, WIDTH), BF16),
            pltpu.VMEM((COLS, PIECE + 8, HID), F32),
            pltpu.VMEM((COLS, PIECE + 8, HID), F32),
            pltpu.VMEM((PIECE + 8, HID), F32),
            pltpu.VMEM((PIECE + 8, HID), F32),
            pltpu.VMEM((YL, PIECE + 8, HID), F32),
            pltpu.VMEM((Z, PIECE + 8, HID), F32),
            pltpu.SemaphoreType.DMA((SCATTER_SENDS,)),
            pltpu.SemaphoreType.DMA((2, 4, YL)),
            pltpu.SemaphoreType.DMA((YL,)),
            pltpu.SemaphoreType.DMA((YL,)),
            pltpu.SemaphoreType.DMA((2, 4)),
            pltpu.SemaphoreType.DMA((COLS,)),
            pltpu.SemaphoreType.DMA((YL,)),
            pltpu.SemaphoreType.DMA((Z,)),
            pltpu.SemaphoreType.DMA((COLS,)),
        ],
        compiler_params=pltpu.CompilerParams(
            collective_id=2, has_side_effects=True, vmem_limit_bytes=VMEM_LIMIT
        ),
    )(partial, gw, gb)


def per_device(features, weight, bias, grad_out, tile_values, tile_rows, tile_cols, tile_count):
    values = tile_values[0, 0]
    slot_rows = tile_rows[0, 0]
    slot_cols = tile_cols[0, 0]
    count = tile_count.reshape(1)
    panel = gather_row(features).reshape(COL_TILES, TILE, WIDTH)
    partial = tile_products(values, slot_cols, slot_rows, count, panel, ROW_TILES, False)
    hidden, block, gw, gb = middle(
        partial.reshape(X, YH, CORE, NODE, WIDTH), grad_out, weight, bias.reshape(1, HID)
    )
    back = tile_products(
        values, slot_rows, slot_cols, count, block.reshape(ROW_TILES, TILE, WIDTH), COL_TILES, True
    )
    grad_features, grad_weight, grad_bias = scatter_row(back.reshape(Z, YL, NODE, WIDTH), gw, gb)
    return hidden, grad_weight.reshape(WIDTH, HID), grad_bias[0], grad_features


def solution(mesh):
    return jax.shard_map(
        per_device,
        mesh=mesh,
        in_specs=(
            P(("col", "row"), None),
            P(),
            P(),
            P(("row", "col"), None),
            P("row", "col", None, None, None),
            P("row", "col", None),
            P("row", "col", None),
            P("row", "col"),
        ),
        out_specs=(P(("row", "col"), None), P(), P(), P(("col", "row"), None)),
        check_vma=False,
    )
```

```python
import functools

import jax
import jax.numpy as jnp
from jax import lax
from jax.experimental import pallas as pl
from jax.experimental.pallas import tpu as pltpu
from jax.sharding import PartitionSpec as P

MESH = pl.DeviceIdType.MESH
F32 = jnp.float32
BF16 = jnp.bfloat16

Z, YL, X, YH, CORE = 8, 4, 4, 2, 2
ROWS, COLS = Z * YL, X * YH * CORE
TILE = 128
NODE = 256
WIDTH = 128
HID = 256
SLOTS = 128
ROW_TILES = COLS * NODE // TILE
COL_TILES = ROWS * NODE // TILE
SPLIT = 192
REST = NODE - SPLIT
VMEM_LIMIT = 56 * 1024 * 1024


def row_of(z, y):
    return z * YL + y


def col_of(x, yh, core):
    return (x * YH + yh) * CORE + core


def where_am_i():
    row = lax.axis_index("row")
    col = lax.axis_index("col")
    return row, col, row // YL, row % YL, col // (YH * CORE), (col // CORE) % YH, col % CORE


def greet(peers):
    barrier = pltpu.get_barrier_semaphore()
    for peer in peers:
        pl.semaphore_signal(barrier, inc=1, device_id=peer, device_id_type=MESH)
    pl.semaphore_wait(barrier, len(peers))


class Sender:
    def __init__(self, sems):
        self.sems = sems
        self.started = []

    def send(self, src, dst, recv_sem, peer):
        copy = pltpu.make_async_remote_copy(
            src_ref=src,
            dst_ref=dst,
            send_sem=self.sems.at[len(self.started)],
            recv_sem=recv_sem,
            device_id=peer,
            device_id_type=MESH,
        )
        copy.start()
        self.started.append(copy)

    def finish(self):
        for copy in self.started:
            copy.wait_send()


def arrived(dst, recv_sem, peer):
    pltpu.make_async_remote_copy(
        src_ref=dst, dst_ref=dst, send_sem=recv_sem, recv_sem=recv_sem, device_id=peer, device_id_type=MESH
    ).wait_recv()


HALF_Z = Z // 2
PIECES = 16
PIECE = WIDTH // PIECES
EXTRA = 8
UNROLL = 16
GATHER_SENDS = 3 + 28 + 7 + 24
MIDDLE_SENDS = 8 + 6 + 1 + 1 + 6 + 8
PARAM_SENDS = 1 + 3 + 1 + 3 + 7 + 1 + 6 + 8
SCATTER_SENDS = 28 + 3
SENDS = GATHER_SENDS + MIDDLE_SENDS + PARAM_SENDS + SCATTER_SENDS


def dot(a, b, ca, cb):
    return lax.dot_general(a, b, (((ca,), (cb,)), ((), ())), preferred_element_type=F32)


def plan(segment, pick, live, last_tile):
    n = SLOTS
    lane = lax.broadcasted_iota(jnp.int32, (n, n), 1)
    sub = lax.broadcasted_iota(jnp.int32, (n, n), 0)
    seg = jnp.where(live, segment, last_tile)
    seg_l = jnp.broadcast_to(seg, (n, n))
    seg_s = seg_l.T
    key_l = seg_l * n + lane
    key_s = seg_s * n + sub
    rank = jnp.sum((key_s < key_l).astype(jnp.int32), axis=0, keepdims=True)
    rank_s = jnp.broadcast_to(rank, (n, n)).T
    hot = (rank_s == lane).astype(jnp.int32)
    pick_s = jnp.broadcast_to(pick, (n, n)).T
    order = jnp.sum(hot * sub, axis=0, keepdims=True)
    picked = jnp.sum(hot * pick_s, axis=0, keepdims=True)
    placed = jnp.sum(hot * seg_s, axis=0, keepdims=True)
    before = jnp.sum((rank_s == lane - 1).astype(jnp.int32) * seg_s, axis=0, keepdims=True)
    keep = jnp.where((placed == before) & (lane[0:1] > 0), 1.0, 0.0)
    upto = jnp.sum((seg_s <= lane).astype(jnp.int32), axis=0, keepdims=True)
    exact = jnp.sum((seg_s == lane).astype(jnp.int32), axis=0, keepdims=True)
    last = jnp.maximum(upto - 1, 0)
    has = jnp.where(exact > 0, 1.0, 0.0)
    return order, picked, last, keep, has


def products(base, ints, floats, values, panel, run, contract):
    def group(g, acc):
        for u in range(UNROLL):
            i = g * UNROLL + u
            slot, tile = ints[base, i], ints[base + 1, i]
            acc = acc * floats[base, i] + dot(values[slot], panel[tile], contract, 0)
            run[i] = acc.astype(BF16)
        return acc

    lax.fori_loop(0, SLOTS // UNROLL, group, jnp.zeros((TILE, WIDTH), F32))


def whole_kernel(
    feat, weight, bias, grad_out, values_hbm, rows_ref, cols_ref, count_ref,
    hidden, gw_out, gb_out, result,
    values, panel, run, partial, paired, pair_in, x_in, y_out, y_in, block, back,
    a_out, a_in, near_out, near_in,
    core_piece, core_piece_in, x_piece, x_piece_in, far_piece, far_piece_in, near_piece, near_piece_in, z_piece, z_piece_in,
    ints_v, floats_v, ints, floats,
    sends, values_sem, table_sem, recv_a, recv_b, pair_sem, x_sem, y_sem, gather_sem, a_sem, near_sem,
    core_psem, x_psem, far_psem, near_psem, z_psem, last_sem,
):
    row, col, z, y, x, yh, core = where_am_i()
    load = pltpu.make_async_copy(values_hbm, values, values_sem)
    load.start()
    up = (row_of((z + 1) % Z, y), col)
    down = (row_of((z + Z - 1) % Z, y), col)
    near = [(row_of(z, (y + j) % YL), col) for j in range(1, YL)]
    along = [(row_of((z + d) % Z, y), col) for d in range(1, Z)]
    sibling = (row, col_of(x, yh, 1 - core))
    far = (row, col_of(x, 1 - yh, core))
    ring = [(row, col_of((x + d) % X, yh, core)) for d in range(1, X)]
    greet(near + along + [sibling, far] + ring)
    out = Sender(sends)

    part_a, part_b = pl.ds(0, SPLIT), pl.ds(SPLIT, REST)

    def shard(dz, j):
        return row_of((z + Z + dz) % Z, (y + j) % YL)

    def a(s):
        return panel.at[s, part_a], recv_a.at[s]

    def b(s):
        return panel.at[s, part_b], recv_b.at[s]

    def pass_on(src, s, way, peer):
        dst, sem = way(s)
        out.send(src, dst, sem, peer)

    mine = feat.at[part_a], feat.at[part_b]
    pass_on(mine[1], row, b, up)
    pass_on(mine[1], row, b, down)
    for j in range(1, YL):
        pass_on(mine[0], row, a, near[j - 1])
    pass_on(mine[0], row, a, up)
    pass_on(mine[0], row, a, down)
    for j in range(1, YL):
        pass_on(mine[1], row, b, near[j - 1])
    panel[row] = feat[...]

    live = lax.broadcasted_iota(jnp.int32, (1, SLOTS), 1) < count_ref[...]
    ints_v[...] = jnp.zeros_like(ints_v)
    floats_v[...] = jnp.zeros_like(floats_v)
    for base, segment, pick, tiles in ((0, rows_ref, cols_ref, ROW_TILES), (3, cols_ref, rows_ref, COL_TILES)):
        order, picked, last, keep, has = plan(segment[...], pick[...], live, tiles)
        ints_v[base:base + 1] = order
        ints_v[base + 1:base + 2] = picked
        ints_v[base + 2:base + 3] = last
        floats_v[base:base + 1] = keep
        floats_v[base + 2:base + 3] = has
    table = [
        pltpu.make_async_copy(ints_v, ints, table_sem.at[0]),
        pltpu.make_async_copy(floats_v, floats, table_sem.at[1]),
    ]
    for copy in table:
        copy.start()

    for j in range(1, YL):
        s = shard(0, j)
        arrived(*a(s), near[j - 1])
        pass_on(a(s)[0], s, a, up)
        pass_on(a(s)[0], s, a, down)
    for d in range(1, HALF_Z):
        for sign, source, target in ((-1, down, up), (1, up, down)):
            s = shard(sign * d, 0)
            arrived(*b(s), source)
            if d < HALF_Z - 1 or sign < 0:
                pass_on(b(s)[0], s, b, target)
            for j in range(1, YL):
                pass_on(b(s)[0], s, b, near[j - 1])
        for j in range(YL):
            for sign, source, target in ((-1, down, up), (1, up, down)):
                s = shard(sign * d, j)
                arrived(*a(s), source)
                if d < HALF_Z - 1 or (j < 2) == (sign < 0):
                    pass_on(a(s)[0], s, a, target)
    s = shard(HALF_Z, 0)
    arrived(*b(s), down)
    for j in range(1, YL):
        pass_on(b(s)[0], s, b, near[j - 1])
    for copy in table:
        copy.wait()
    load.wait()
    for j in range(YL):
        arrived(*a(shard(HALF_Z, j)), down if j < 2 else up)
    for dz in range(Z):
        for j in range(1, YL):
            arrived(*b(shard(dz, j)), near[j - 1])

    products(0, ints, floats, values, panel.reshape(COL_TILES, TILE, WIDTH), run, 1)
    tiles_per = NODE // TILE
    for r in range(ROW_TILES):
        c, t = r // tiles_per, r % tiles_per
        tile = (run[ints[2, r]].astype(F32) * floats[2, r]).astype(BF16)
        partial[c // (YH * CORE), (c // CORE) % YH, c % CORE, t * TILE:(t + 1) * TILE] = tile

    order = [2, 1, 3, 0]
    for h in range(YH):
        hh = (1 - yh) if h == 0 else yh
        for d in order:
            other = (x + d) % X
            out.send(partial.at[other, hh, 1 - core], pair_in.at[h, d], pair_sem.at[h, d], sibling)
    for h in range(YH):
        hh = (1 - yh) if h == 0 else yh
        for d in order:
            other = (x + d) % X
            arrived(pair_in.at[h, d], pair_sem.at[h, d], sibling)
            paired[h, d] = (partial[other, hh, core].astype(F32) + pair_in[h, d].astype(F32)).astype(BF16)
            if d:
                out.send(paired.at[h, d], x_in.at[h, X - d], x_sem.at[h, X - d], ring[d - 1])

    def summed(h):
        acc = paired[h, 0].astype(F32)
        for d in range(1, X):
            arrived(x_in.at[h, d], x_sem.at[h, d], ring[d - 1])
            acc += x_in[h, d].astype(F32)
        return acc

    y_out[...] = summed(0).astype(BF16)
    out.send(y_out, y_in, y_sem.at[0], far)
    own = summed(1)
    arrived(y_in, y_sem.at[0], far)
    aggregate = (own + y_in[...].astype(F32)).astype(BF16)

    preact = jnp.dot(aggregate, weight[...], preferred_element_type=F32) + bias[...]
    sigmoid = jax.nn.sigmoid(preact)
    slope = sigmoid * (1.0 + preact * (1.0 - sigmoid))
    grad_pre = (grad_out[...].astype(F32) * slope).astype(BF16)
    block[col] = dot(grad_pre, weight[...], 1, 1).astype(BF16)

    def g(c):
        return block.at[c], gather_sem.at[c]

    def share(c, peer):
        out.send(block.at[c], block.at[c], gather_sem.at[c], peer)

    share(col, far)
    for d in order[:3]:
        share(col, ring[d - 1])
    share(col, sibling)
    hidden[...] = (preact * sigmoid).astype(BF16)
    gw = dot(aggregate, grad_pre, 0, 0)
    gb = jnp.broadcast_to(jnp.sum(grad_pre.astype(F32), axis=0, keepdims=True), (EXTRA, HID))
    half = WIDTH // CORE
    for c in range(CORE):
        core_piece[c, :half] = gw[c * half:(c + 1) * half]
        core_piece[c, half:] = gb
    out.send(core_piece.at[1 - core], core_piece_in, core_psem.at[0], sibling)
    c = col_of(x, 1 - yh, core)
    arrived(*g(c), far)
    for d in order[:3]:
        share(c, ring[d - 1])
    share(c, sibling)
    arrived(core_piece_in, core_psem.at[0], sibling)
    quarter = half // X
    for q in range(X):
        for here, size, at in ((q * quarter, quarter, 0), (half, EXTRA, quarter)):
            x_piece[q, at:at + size] = core_piece[core, here:here + size] + core_piece_in[here:here + size]
    for d in range(1, X):
        out.send(x_piece.at[(x + d) % X], x_piece_in.at[X - d], x_psem.at[X - d], ring[d - 1])
    for d in (1, 3, 2):
        for h in (yh, 1 - yh):
            c = col_of((x + d) % X, h, core)
            arrived(*g(c), ring[d - 1])
            share(c, sibling)
    acc = x_piece[x]
    for d in range(1, X):
        arrived(x_piece_in.at[d], x_psem.at[d], ring[d - 1])
        acc = acc + x_piece_in[d]
    for h in range(YH):
        far_piece[h, :PIECE] = acc[h * PIECE:(h + 1) * PIECE]
        far_piece[h, PIECE:] = acc[quarter:]
    out.send(far_piece.at[1 - yh], far_piece_in, far_psem.at[0], far)
    for d in range(X):
        for h in range(YH):
            arrived(*g(col_of((x + d) % X, h, 1 - core)), sibling)

    products(3, ints, floats, values, block.reshape(ROW_TILES, TILE, WIDTH), run, 0)
    for r in range(COL_TILES):
        s, t = r // tiles_per, r % tiles_per
        tile = (run[ints[5, r]].astype(F32) * floats[5, r]).astype(BF16)
        back[s // YL, s % YL, t * TILE:(t + 1) * TILE] = tile

    ways = ((0, 1, up, down), (1, -1, down, up))
    turns = (1, 2, 3, 0)

    def own_a(dz, j):
        return back.at[(z + Z + dz) % Z, (y + j) % YL]

    for j in turns:
        way, _, target, _ = ways[0] if j < 2 else ways[1]
        out.send(own_a(HALF_Z, j), a_in.at[way, 0, j], a_sem.at[way, 0, j], target)
    for j in turns:
        way, sign, target, _ = ways[1] if j < 2 else ways[0]
        out.send(own_a(sign * (HALF_Z - 1), j), a_in.at[way, 1, j], a_sem.at[way, 1, j], target)
    arrived(far_piece_in, far_psem.at[0], far)
    near_piece[...] = far_piece[yh] + far_piece_in[...]
    for j in range(1, YL):
        out.send(near_piece, near_piece_in.at[YL - j], near_psem.at[YL - j], near[j - 1])

    def hop(step, j, way, sign, target, source):
        arrived(a_in.at[way, step - 1, j], a_sem.at[way, step - 1, j], source)
        a_out[way, step, j] = (
            own_a(sign * (HALF_Z - step), j)[...].astype(F32) + a_in[way, step - 1, j].astype(F32)
        ).astype(BF16)
        out.send(a_out.at[way, step, j], a_in.at[way, step, j], a_sem.at[way, step, j], target)

    for j in turns:
        hop(1, j, *(ways[0] if j < 2 else ways[1]))
    acc = near_piece[...]
    for j in range(1, YL):
        arrived(near_piece_in.at[j], near_psem.at[j], near[j - 1])
        acc = acc + near_piece_in[j]
    z_piece[...] = acc
    for d in range(1, Z):
        out.send(z_piece, z_piece_in.at[Z - d], z_psem.at[Z - d], along[d - 1])
    for j in turns:
        for way in ways:
            hop(2, j, *way)
    acc = z_piece[...]
    for d in range(1, Z):
        arrived(z_piece_in.at[d], z_psem.at[d], along[d - 1])
        acc = acc + z_piece_in[d]

    def spot(x_at, h, c):
        return (c * X + x_at) * YH + h

    def last(p):
        return gw_out.at[p], last_sem.at[p]

    def spread(p, peer):
        out.send(gw_out.at[p], gw_out.at[p], last_sem.at[p], peer)

    gw_out[spot(x, yh, core)] = acc[:PIECE]
    gb_out[...] = acc[PIECE:]
    spread(spot(x, yh, core), far)
    for d in range(1, X):
        spread(spot(x, yh, core), ring[d - 1])
    spread(spot(x, yh, core), sibling)
    for j in turns:
        for way in ways:
            hop(3, j, *way)
    p = spot(x, 1 - yh, core)
    arrived(*last(p), far)
    for d in range(1, X):
        spread(p, ring[d - 1])
    spread(p, sibling)

    def final_a(j):
        acc = own_a(0, j)[...].astype(F32)
        for way, _, _, source in ways:
            arrived(a_in.at[way, 3, j], a_sem.at[way, 3, j], source)
            acc += a_in[way, 3, j].astype(F32)
        return acc

    for j in range(1, YL):
        near_out[j] = final_a(j).astype(BF16)
        out.send(near_out.at[j], near_in.at[YL - j], near_sem.at[YL - j], near[j - 1])
    for d in range(1, X):
        for h in (yh, 1 - yh):
            p = spot((x + d) % X, h, core)
            arrived(*last(p), ring[d - 1])
            spread(p, sibling)
    total = final_a(0)
    for j in range(1, YL):
        arrived(near_in.at[j], near_sem.at[j], near[j - 1])
        total += near_in[j].astype(F32)
    result[...] = total.astype(BF16)
    for d in range(X):
        for h in range(YH):
            arrived(*last(spot((x + d) % X, h, 1 - core)), sibling)
    out.finish()


def whole(features, weight, bias, grad_out, values, rows, cols, count):
    vmem = pl.BlockSpec(memory_space=pltpu.VMEM)
    dma = pltpu.SemaphoreType.DMA
    return pl.pallas_call(
        whole_kernel,
        out_shape=(
            jax.ShapeDtypeStruct((NODE, HID), BF16),
            jax.ShapeDtypeStruct((PIECES, PIECE, HID), F32),
            jax.ShapeDtypeStruct((EXTRA, HID), F32),
            jax.ShapeDtypeStruct((NODE, WIDTH), BF16),
        ),
        in_specs=[vmem] * 4 + [pl.BlockSpec(memory_space=pl.ANY)] + [vmem] * 3,
        out_specs=(vmem,) * 4,
        scratch_shapes=[
            pltpu.VMEM((SLOTS, TILE, TILE), BF16),
            pltpu.VMEM((ROWS, NODE, WIDTH), BF16),
            pltpu.VMEM((SLOTS, TILE, WIDTH), BF16),
            pltpu.VMEM((X, YH, CORE, NODE, WIDTH), BF16),
            pltpu.VMEM((YH, X, NODE, WIDTH), BF16),
            pltpu.VMEM((YH, X, NODE, WIDTH), BF16),
            pltpu.VMEM((YH, X, NODE, WIDTH), BF16),
            pltpu.VMEM((NODE, WIDTH), BF16),
            pltpu.VMEM((NODE, WIDTH), BF16),
            pltpu.VMEM((COLS, NODE, WIDTH), BF16),
            pltpu.VMEM((Z, YL, NODE, WIDTH), BF16),
            pltpu.VMEM((2, 4, YL, NODE, WIDTH), BF16),
            pltpu.VMEM((2, 4, YL, NODE, WIDTH), BF16),
            pltpu.VMEM((YL, NODE, WIDTH), BF16),
            pltpu.VMEM((YL, NODE, WIDTH), BF16),
            pltpu.VMEM((CORE, WIDTH // CORE + EXTRA, HID), F32),
            pltpu.VMEM((WIDTH // CORE + EXTRA, HID), F32),
            pltpu.VMEM((X, WIDTH // CORE // X + EXTRA, HID), F32),
            pltpu.VMEM((X, WIDTH // CORE // X + EXTRA, HID), F32),
            pltpu.VMEM((YH, PIECE + EXTRA, HID), F32),
            pltpu.VMEM((PIECE + EXTRA, HID), F32),
            pltpu.VMEM((PIECE + EXTRA, HID), F32),
            pltpu.VMEM((YL, PIECE + EXTRA, HID), F32),
            pltpu.VMEM((PIECE + EXTRA, HID), F32),
            pltpu.VMEM((Z, PIECE + EXTRA, HID), F32),
            pltpu.VMEM((8, SLOTS), jnp.int32),
            pltpu.VMEM((8, SLOTS), F32),
            pltpu.SMEM((8, SLOTS), jnp.int32),
            pltpu.SMEM((8, SLOTS), F32),
            dma((SENDS,)),
            dma,
            dma((2,)),
            dma((ROWS,)),
            dma((ROWS,)),
            dma((YH, X)),
            dma((YH, X)),
            dma((1,)),
            dma((COLS,)),
            dma((2, 4, YL)),
            dma((YL,)),
            dma((1,)),
            dma((X,)),
            dma((1,)),
            dma((YL,)),
            dma((Z,)),
            dma((PIECES,)),
        ],
        compiler_params=pltpu.CompilerParams(
            collective_id=0, has_side_effects=True, vmem_limit_bytes=VMEM_LIMIT
        ),
    )(features, weight, bias, grad_out, values, rows, cols, count)


def finish_kernel(hidden, gw, gb, result, hidden_out, gw_out, gb_out, result_out):
    hidden_out[...] = hidden[...]
    gw_out[...] = gw[...]
    gb_out[...] = gb[0:1]
    result_out[...] = result[...]


def finish(hidden, gw, gb, result):
    vmem = pl.BlockSpec(memory_space=pltpu.VMEM)
    return pl.pallas_call(
        finish_kernel,
        out_shape=(
            jax.ShapeDtypeStruct((NODE, HID), BF16),
            jax.ShapeDtypeStruct((WIDTH, HID), F32),
            jax.ShapeDtypeStruct((1, HID), F32),
            jax.ShapeDtypeStruct((NODE, WIDTH), BF16),
        ),
        in_specs=[vmem] * 4,
        out_specs=(vmem,) * 4,
    )(hidden, gw, gb, result)


def split_rows(outs):
    hidden, gw, gb, result = outs
    return hidden, gw.reshape(WIDTH, HID), gb, result


def per_device(features, weight, bias, grad_out, tile_values, tile_rows, tile_cols, tile_count):
    hidden, grad_weight, grad_bias, grad_features = finish(*split_rows(whole(
        features, weight, bias.reshape(1, HID), grad_out, tile_values[0, 0], tile_rows[0], tile_cols[0], tile_count
    )))
    return hidden, grad_weight, grad_bias[0], grad_features


def solution(mesh):
    return jax.shard_map(
        per_device,
        mesh=mesh,
        in_specs=(
            P(("col", "row"), None),
            P(),
            P(),
            P(("row", "col"), None),
            P("row", "col", None, None, None),
            P("row", "col", None),
            P("row", "col", None),
            P("row", "col"),
        ),
        out_specs=(P(("row", "col"), None), P(), P(), P(("col", "row"), None)),
        check_vma=False,
    )
```

```python
import functools

import jax
import jax.numpy as jnp
from jax import lax
from jax.experimental import pallas as pl
from jax.experimental.pallas import tpu as pltpu
from jax.sharding import PartitionSpec as P

MESH = pl.DeviceIdType.MESH
F32 = jnp.float32
BF16 = jnp.bfloat16

Z, YL, X, YH, CORE = 8, 4, 4, 2, 2
ROWS, COLS = Z * YL, X * YH * CORE
TILE = 128
NODE = 256
WIDTH = 128
HID = 256
SLOTS = 128
ROW_TILES = COLS * NODE // TILE
COL_TILES = ROWS * NODE // TILE
SPLIT = 144
REST = NODE - SPLIT
VMEM_LIMIT = 56 * 1024 * 1024


def row_of(z, y):
    return z * YL + y


def col_of(x, yh, core):
    return (x * YH + yh) * CORE + core


def where_am_i():
    row = lax.axis_index("row")
    col = lax.axis_index("col")
    return row, col, row // YL, row % YL, col // (YH * CORE), (col // CORE) % YH, col % CORE


def greet(peers):
    barrier = pltpu.get_barrier_semaphore()
    for peer in peers:
        pl.semaphore_signal(barrier, inc=1, device_id=peer, device_id_type=MESH)
    pl.semaphore_wait(barrier, len(peers))


class Sender:
    def __init__(self, sems):
        self.sems = sems
        self.started = []
        self.waited = 0

    def send(self, src, dst, recv_sem, peer):
        copy = pltpu.make_async_remote_copy(
            src_ref=src,
            dst_ref=dst,
            send_sem=self.sems.at[len(self.started)],
            recv_sem=recv_sem,
            device_id=peer,
            device_id_type=MESH,
        )
        copy.start()
        self.started.append(copy)

    def finish(self, upto=None):
        for copy in self.started[self.waited:upto]:
            copy.wait_send()
        self.waited = len(self.started) if upto is None else upto


def arrived(dst, recv_sem, peer):
    pltpu.make_async_remote_copy(
        src_ref=dst, dst_ref=dst, send_sem=recv_sem, recv_sem=recv_sem, device_id=peer, device_id_type=MESH
    ).wait_recv()


HALF_Z = Z // 2
PIECES = 16
PIECE = WIDTH // PIECES
EXTRA = 8
UNROLL = 32
GATHER_SENDS = 3 + 28 + 7 + 24
MIDDLE_SENDS = 8 + 6 + 1 + 1 + 6 + 8
PARAM_SENDS = 1 + 3 + 1 + 3 + 7 + 1 + 6 + 8
SCATTER_SENDS = 28 + 3
SENDS = GATHER_SENDS + MIDDLE_SENDS + PARAM_SENDS + SCATTER_SENDS


def dot(a, b, ca, cb):
    return lax.dot_general(a, b, (((ca,), (cb,)), ((), ())), preferred_element_type=F32)


def plan(segment, pick, live, last_tile):
    n = SLOTS
    lane = lax.broadcasted_iota(jnp.int32, (n, n), 1)
    sub = lax.broadcasted_iota(jnp.int32, (n, n), 0)
    seg = jnp.where(live, segment, last_tile)
    seg_l = jnp.broadcast_to(seg, (n, n))
    seg_s = seg_l.T
    key_l = seg_l * n + lane
    key_s = seg_s * n + sub
    rank = jnp.sum((key_s < key_l).astype(jnp.int32), axis=0, keepdims=True)
    rank_s = jnp.broadcast_to(rank, (n, n)).T
    hot = (rank_s == lane).astype(jnp.int32)
    pick_s = jnp.broadcast_to(pick, (n, n)).T
    order = jnp.sum(hot * sub, axis=0, keepdims=True)
    picked = jnp.sum(hot * pick_s, axis=0, keepdims=True)
    placed = jnp.sum(hot * seg_s, axis=0, keepdims=True)
    before = jnp.sum((rank_s == lane - 1).astype(jnp.int32) * seg_s, axis=0, keepdims=True)
    keep = jnp.where((placed == before) & (lane[0:1] > 0), 1.0, 0.0)
    upto = jnp.sum((seg_s <= lane).astype(jnp.int32), axis=0, keepdims=True)
    exact = jnp.sum((seg_s == lane).astype(jnp.int32), axis=0, keepdims=True)
    last = jnp.maximum(upto - 1, 0)
    has = jnp.where(exact > 0, 1.0, 0.0)
    return order, picked, last, keep, has


def products(base, ints, floats, values, panel, run, contract):
    def group(g, acc):
        for u in range(UNROLL):
            i = g * UNROLL + u
            slot, tile = ints[base, i], ints[base + 1, i]
            acc = acc * floats[base, i] + dot(values[slot], panel[tile], contract, 0)
            run[i] = acc.astype(BF16)
        return acc

    lax.fori_loop(0, SLOTS // UNROLL, group, jnp.zeros((TILE, WIDTH), F32))


def whole_kernel(
    feat, weight, bias, grad_out, values_hbm, rows_ref, cols_ref, count_ref,
    hidden, gw_out, gb_out, result,
    values, panel, run, partial, paired, pair_in, x_in, y_out, y_in, block, back,
    a_out, a_in, near_out, near_in,
    core_piece, core_piece_in, x_piece, x_piece_in, far_piece, far_piece_in, near_piece, near_piece_in, z_piece, z_piece_in,
    ints_v, floats_v, ints, floats,
    sends, values_sem, table_sem, recv_a, recv_b, pair_sem, x_sem, y_sem, gather_sem, a_sem, near_sem,
    core_psem, x_psem, far_psem, near_psem, z_psem, last_sem,
):
    row, col, z, y, x, yh, core = where_am_i()
    load = pltpu.make_async_copy(values_hbm, values, values_sem)
    load.start()
    up = (row_of((z + 1) % Z, y), col)
    down = (row_of((z + Z - 1) % Z, y), col)
    near = [(row_of(z, (y + j) % YL), col) for j in range(1, YL)]
    along = [(row_of((z + d) % Z, y), col) for d in range(1, Z)]
    sibling = (row, col_of(x, yh, 1 - core))
    far = (row, col_of(x, 1 - yh, core))
    ring = [(row, col_of((x + d) % X, yh, core)) for d in range(1, X)]
    greet(near + along + [sibling, far] + ring)
    out = Sender(sends)

    part_a, part_b = pl.ds(0, SPLIT), pl.ds(SPLIT, REST)

    def shard(dz, j):
        return row_of((z + Z + dz) % Z, (y + j) % YL)

    def a(s):
        return panel.at[s, part_a], recv_a.at[s]

    def b(s):
        return panel.at[s, part_b], recv_b.at[s]

    def pass_on(src, s, way, peer):
        dst, sem = way(s)
        out.send(src, dst, sem, peer)

    mine = feat.at[part_a], feat.at[part_b]
    pass_on(mine[1], row, b, up)
    pass_on(mine[1], row, b, down)
    for j in range(1, YL):
        pass_on(mine[0], row, a, near[j - 1])
    pass_on(mine[0], row, a, up)
    pass_on(mine[0], row, a, down)
    for j in range(1, YL):
        pass_on(mine[1], row, b, near[j - 1])
    panel[row] = feat[...]

    live = lax.broadcasted_iota(jnp.int32, (1, SLOTS), 1) < count_ref[...]
    ints_v[...] = jnp.zeros_like(ints_v)
    floats_v[...] = jnp.zeros_like(floats_v)
    for base, segment, pick, tiles in ((0, rows_ref, cols_ref, ROW_TILES), (3, cols_ref, rows_ref, COL_TILES)):
        order, picked, last, keep, has = plan(segment[...], pick[...], live, tiles)
        ints_v[base:base + 1] = order
        ints_v[base + 1:base + 2] = picked
        ints_v[base + 2:base + 3] = last
        floats_v[base:base + 1] = keep
        floats_v[base + 2:base + 3] = has
    table = [
        pltpu.make_async_copy(ints_v, ints, table_sem.at[0]),
        pltpu.make_async_copy(floats_v, floats, table_sem.at[1]),
    ]
    for copy in table:
        copy.start()

    for j in range(1, YL):
        s = shard(0, j)
        arrived(*a(s), near[j - 1])
        pass_on(a(s)[0], s, a, up)
        pass_on(a(s)[0], s, a, down)
    for d in range(1, HALF_Z):
        for sign, source, target in ((-1, down, up), (1, up, down)):
            s = shard(sign * d, 0)
            arrived(*b(s), source)
            if d < HALF_Z - 1 or sign < 0:
                pass_on(b(s)[0], s, b, target)
            for j in range(1, YL):
                pass_on(b(s)[0], s, b, near[j - 1])
        for j in range(YL):
            for sign, source, target in ((-1, down, up), (1, up, down)):
                s = shard(sign * d, j)
                arrived(*a(s), source)
                if d < HALF_Z - 1 or (j < 2) == (sign < 0):
                    pass_on(a(s)[0], s, a, target)
    s = shard(HALF_Z, 0)
    arrived(*b(s), down)
    for j in range(1, YL):
        pass_on(b(s)[0], s, b, near[j - 1])
    for copy in table:
        copy.wait()
    load.wait()
    for j in range(YL):
        arrived(*a(shard(HALF_Z, j)), down if j < 2 else up)
    for dz in range(Z):
        for j in range(1, YL):
            arrived(*b(shard(dz, j)), near[j - 1])

    products(0, ints, floats, values, panel.reshape(COL_TILES, TILE, WIDTH), run, 1)
    tiles_per = NODE // TILE
    gathered = len(out.started)
    order = [2, 1, 3, 0]

    def result_tile(base, r):
        return (run[ints[base, r]].astype(F32) * floats[base, r]).astype(BF16)

    for c in (1 - core, core):
        for h in range(YH):
            hh = (1 - yh) if h == 0 else yh
            for d in order:
                other = (x + d) % X
                for t in range(tiles_per):
                    partial[other, hh, c, t * TILE:(t + 1) * TILE] = result_tile(2, col_of(other, hh, c) * tiles_per + t)
                if c is not core:
                    out.send(partial.at[other, hh, c], pair_in.at[h, d], pair_sem.at[h, d], sibling)
    for h in range(YH):
        hh = (1 - yh) if h == 0 else yh
        for d in order:
            other = (x + d) % X
            arrived(pair_in.at[h, d], pair_sem.at[h, d], sibling)
            paired[h, d] = (partial[other, hh, core].astype(F32) + pair_in[h, d].astype(F32)).astype(BF16)
            if d:
                out.send(paired.at[h, d], x_in.at[h, X - d], x_sem.at[h, X - d], ring[d - 1])

    def summed(h):
        acc = paired[h, 0].astype(F32)
        for d in range(1, X):
            arrived(x_in.at[h, d], x_sem.at[h, d], ring[d - 1])
            acc += x_in[h, d].astype(F32)
        return acc

    out.finish(gathered)
    y_out[...] = summed(0).astype(BF16)
    out.send(y_out, y_in, y_sem.at[0], far)
    own = summed(1)
    arrived(y_in, y_sem.at[0], far)
    aggregate = (own + y_in[...].astype(F32)).astype(BF16)

    preact = jnp.dot(aggregate, weight[...], preferred_element_type=F32) + bias[...]
    sigmoid = jax.nn.sigmoid(preact)
    slope = sigmoid * (1.0 + preact * (1.0 - sigmoid))
    grad_pre = (grad_out[...].astype(F32) * slope).astype(BF16)
    block[col] = dot(grad_pre, weight[...], 1, 1).astype(BF16)

    def g(c):
        return block.at[c], gather_sem.at[c]

    def share(c, peer):
        out.send(block.at[c], block.at[c], gather_sem.at[c], peer)

    share(col, far)
    for d in order[:3]:
        share(col, ring[d - 1])
    share(col, sibling)
    hidden[...] = (preact * sigmoid).astype(BF16)
    gw = dot(aggregate, grad_pre, 0, 0)
    gb = jnp.broadcast_to(jnp.sum(grad_pre.astype(F32), axis=0, keepdims=True), (EXTRA, HID))
    half = WIDTH // CORE
    for c in range(CORE):
        core_piece[c, :half] = gw[c * half:(c + 1) * half]
        core_piece[c, half:] = gb
    out.send(core_piece.at[1 - core], core_piece_in, core_psem.at[0], sibling)
    out.finish(len(out.started) - 6)
    arrived(core_piece_in, core_psem.at[0], sibling)
    quarter = half // X
    for q in range(X):
        for here, size, at in ((q * quarter, quarter, 0), (half, EXTRA, quarter)):
            x_piece[q, at:at + size] = core_piece[core, here:here + size] + core_piece_in[here:here + size]
    for d in range(1, X):
        out.send(x_piece.at[(x + d) % X], x_piece_in.at[X - d], x_psem.at[X - d], ring[d - 1])

    def from_ring(d, h):
        c = col_of((x + d) % X, h, core)
        arrived(*g(c), ring[d - 1])
        share(c, sibling)

    from_ring(1, yh)
    from_ring(3, yh)
    c = col_of(x, 1 - yh, core)
    arrived(*g(c), far)
    for d in order[:3]:
        share(c, ring[d - 1])
    share(c, sibling)
    from_ring(2, yh)
    acc = x_piece[x]
    for d in range(1, X):
        arrived(x_piece_in.at[d], x_psem.at[d], ring[d - 1])
        acc = acc + x_piece_in[d]
    z_piece[...] = acc
    for d in range(1, Z):
        out.send(z_piece, z_piece_in.at[Z - d], z_psem.at[Z - d], along[d - 1])
    for d in (1, 3, 2):
        from_ring(d, 1 - yh)
    for d in range(X):
        for h in range(YH):
            arrived(*g(col_of((x + d) % X, h, 1 - core)), sibling)

    products(3, ints, floats, values, block.reshape(ROW_TILES, TILE, WIDTH), run, 0)
    gathered = len(out.started)

    ways = ((0, 1, up, down), (1, -1, down, up))
    turns = (1, 2, 3, 0)

    def own_a(dz, j):
        return back.at[(z + Z + dz) % Z, (y + j) % YL]

    def build(dz, j):
        zz, yy = (z + Z + dz) % Z, (y + j) % YL
        for t in range(tiles_per):
            back[zz, yy, t * TILE:(t + 1) * TILE] = result_tile(5, row_of(zz, yy) * tiles_per + t)

    def begin(step, j, way, sign, target, source):
        build(sign * (HALF_Z - step), j)
        out.send(own_a(sign * (HALF_Z - step), j), a_in.at[way, step, j], a_sem.at[way, step, j], target)

    for j in (1, 2):
        begin(0, j, *(ways[0] if j < 2 else ways[1]))
    for j in (3, 0):
        begin(0, j, *(ways[0] if j < 2 else ways[1]))
    for j in turns:
        begin(1, j, *(ways[1] if j < 2 else ways[0]))
    for j in turns:
        build(HALF_Z - 1 if j < 2 else 1 - HALF_Z, j)
    acc = z_piece[...]
    for d in range(1, Z):
        arrived(z_piece_in.at[d], z_psem.at[d], along[d - 1])
        acc = acc + z_piece_in[d]
    for h in range(YH):
        far_piece[h, :PIECE] = acc[h * PIECE:(h + 1) * PIECE]
        far_piece[h, PIECE:] = acc[quarter:]
    out.send(far_piece.at[1 - yh], far_piece_in, far_psem.at[0], far)
    for dz in (2, -2):
        for j in turns:
            build(dz, j)

    def hop(step, j, way, sign, target, source):
        arrived(a_in.at[way, step - 1, j], a_sem.at[way, step - 1, j], source)
        a_out[way, step, j] = (
            own_a(sign * (HALF_Z - step), j)[...].astype(F32) + a_in[way, step - 1, j].astype(F32)
        ).astype(BF16)
        out.send(a_out.at[way, step, j], a_in.at[way, step, j], a_sem.at[way, step, j], target)

    for j in turns:
        hop(1, j, *(ways[0] if j < 2 else ways[1]))
    for dz in (1, -1, 0):
        for j in turns:
            build(dz, j)
    out.finish(gathered)
    arrived(far_piece_in, far_psem.at[0], far)
    near_piece[...] = far_piece[yh] + far_piece_in[...]
    for j in range(1, YL):
        out.send(near_piece, near_piece_in.at[YL - j], near_psem.at[YL - j], near[j - 1])
    for j in turns:
        for way in ways:
            hop(2, j, *way)
    acc = near_piece[...]
    for j in range(1, YL):
        arrived(near_piece_in.at[j], near_psem.at[j], near[j - 1])
        acc = acc + near_piece_in[j]

    def spot(x_at, h, c):
        return (c * X + x_at) * YH + h

    def last(p):
        return gw_out.at[p], last_sem.at[p]

    def spread(p, peer):
        out.send(gw_out.at[p], gw_out.at[p], last_sem.at[p], peer)

    gw_out[spot(x, yh, core)] = acc[:PIECE]
    gb_out[...] = acc[PIECE:]
    spread(spot(x, yh, core), far)
    for d in range(1, X):
        spread(spot(x, yh, core), ring[d - 1])
    spread(spot(x, yh, core), sibling)
    for j in turns:
        for way in ways:
            hop(3, j, *way)
    out.finish(len(out.started) - 16)
    p = spot(x, 1 - yh, core)
    arrived(*last(p), far)
    for d in range(1, X):
        spread(p, ring[d - 1])
    spread(p, sibling)

    def final_a(j):
        acc = own_a(0, j)[...].astype(F32)
        for way, _, _, source in ways:
            arrived(a_in.at[way, 3, j], a_sem.at[way, 3, j], source)
            acc += a_in[way, 3, j].astype(F32)
        return acc

    for j in range(1, YL):
        near_out[j] = final_a(j).astype(BF16)
        out.send(near_out.at[j], near_in.at[YL - j], near_sem.at[YL - j], near[j - 1])
    for d in range(1, X):
        for h in (yh, 1 - yh):
            p = spot((x + d) % X, h, core)
            arrived(*last(p), ring[d - 1])
            spread(p, sibling)
    total = final_a(0)
    for j in range(1, YL):
        arrived(near_in.at[j], near_sem.at[j], near[j - 1])
        total += near_in[j].astype(F32)
    result[...] = total.astype(BF16)
    for d in range(X):
        for h in range(YH):
            arrived(*last(spot((x + d) % X, h, 1 - core)), sibling)
    out.finish()


def whole(features, weight, bias, grad_out, values, rows, cols, count):
    vmem = pl.BlockSpec(memory_space=pltpu.VMEM)
    dma = pltpu.SemaphoreType.DMA
    return pl.pallas_call(
        whole_kernel,
        out_shape=(
            jax.ShapeDtypeStruct((NODE, HID), BF16),
            jax.ShapeDtypeStruct((PIECES, PIECE, HID), F32),
            jax.ShapeDtypeStruct((EXTRA, HID), F32),
            jax.ShapeDtypeStruct((NODE, WIDTH), BF16),
        ),
        in_specs=[vmem] * 4 + [pl.BlockSpec(memory_space=pl.ANY)] + [vmem] * 3,
        out_specs=(vmem,) * 4,
        scratch_shapes=[
            pltpu.VMEM((SLOTS, TILE, TILE), BF16),
            pltpu.VMEM((ROWS, NODE, WIDTH), BF16),
            pltpu.VMEM((SLOTS, TILE, WIDTH), BF16),
            pltpu.VMEM((X, YH, CORE, NODE, WIDTH), BF16),
            pltpu.VMEM((YH, X, NODE, WIDTH), BF16),
            pltpu.VMEM((YH, X, NODE, WIDTH), BF16),
            pltpu.VMEM((YH, X, NODE, WIDTH), BF16),
            pltpu.VMEM((NODE, WIDTH), BF16),
            pltpu.VMEM((NODE, WIDTH), BF16),
            pltpu.VMEM((COLS, NODE, WIDTH), BF16),
            pltpu.VMEM((Z, YL, NODE, WIDTH), BF16),
            pltpu.VMEM((2, 4, YL, NODE, WIDTH), BF16),
            pltpu.VMEM((2, 4, YL, NODE, WIDTH), BF16),
            pltpu.VMEM((YL, NODE, WIDTH), BF16),
            pltpu.VMEM((YL, NODE, WIDTH), BF16),
            pltpu.VMEM((CORE, WIDTH // CORE + EXTRA, HID), F32),
            pltpu.VMEM((WIDTH // CORE + EXTRA, HID), F32),
            pltpu.VMEM((X, WIDTH // CORE // X + EXTRA, HID), F32),
            pltpu.VMEM((X, WIDTH // CORE // X + EXTRA, HID), F32),
            pltpu.VMEM((YH, PIECE + EXTRA, HID), F32),
            pltpu.VMEM((PIECE + EXTRA, HID), F32),
            pltpu.VMEM((PIECE + EXTRA, HID), F32),
            pltpu.VMEM((YL, PIECE + EXTRA, HID), F32),
            pltpu.VMEM((WIDTH // CORE // X + EXTRA, HID), F32),
            pltpu.VMEM((Z, WIDTH // CORE // X + EXTRA, HID), F32),
            pltpu.VMEM((8, SLOTS), jnp.int32),
            pltpu.VMEM((8, SLOTS), F32),
            pltpu.SMEM((8, SLOTS), jnp.int32),
            pltpu.SMEM((8, SLOTS), F32),
            dma((SENDS,)),
            dma,
            dma((2,)),
            dma((ROWS,)),
            dma((ROWS,)),
            dma((YH, X)),
            dma((YH, X)),
            dma((1,)),
            dma((COLS,)),
            dma((2, 4, YL)),
            dma((YL,)),
            dma((1,)),
            dma((X,)),
            dma((1,)),
            dma((YL,)),
            dma((Z,)),
            dma((PIECES,)),
        ],
        compiler_params=pltpu.CompilerParams(
            collective_id=0, has_side_effects=True, vmem_limit_bytes=VMEM_LIMIT
        ),
    )(features, weight, bias, grad_out, values, rows, cols, count)


def finish_kernel(hidden, gw, gb, result, hidden_out, gw_out, gb_out, result_out):
    hidden_out[...] = hidden[...]
    gw_out[...] = gw[...]
    gb_out[...] = gb[0:1]
    result_out[...] = result[...]


def finish(hidden, gw, gb, result):
    vmem = pl.BlockSpec(memory_space=pltpu.VMEM)
    return pl.pallas_call(
        finish_kernel,
        out_shape=(
            jax.ShapeDtypeStruct((NODE, HID), BF16),
            jax.ShapeDtypeStruct((WIDTH, HID), F32),
            jax.ShapeDtypeStruct((1, HID), F32),
            jax.ShapeDtypeStruct((NODE, WIDTH), BF16),
        ),
        in_specs=[vmem] * 4,
        out_specs=(vmem,) * 4,
    )(hidden, gw, gb, result)


def split_rows(outs):
    hidden, gw, gb, result = outs
    return hidden, gw.reshape(WIDTH, HID), gb, result


def per_device(features, weight, bias, grad_out, tile_values, tile_rows, tile_cols, tile_count):
    hidden, grad_weight, grad_bias, grad_features = finish(*split_rows(whole(
        features, weight, bias.reshape(1, HID), grad_out, tile_values[0, 0], tile_rows[0], tile_cols[0], tile_count
    )))
    return hidden, grad_weight, grad_bias[0], grad_features


def solution(mesh):
    return jax.shard_map(
        per_device,
        mesh=mesh,
        in_specs=(
            P(("col", "row"), None),
            P(),
            P(),
            P(("row", "col"), None),
            P("row", "col", None, None, None),
            P("row", "col", None),
            P("row", "col", None),
            P("row", "col"),
        ),
        out_specs=(P(("row", "col"), None), P(), P(), P(("col", "row"), None)),
        check_vma=False,
    )
```

```python
import functools

import jax
import jax.numpy as jnp
from jax import lax
from jax.experimental import pallas as pl
from jax.experimental.pallas import tpu as pltpu
from jax.sharding import PartitionSpec as P

MESH = pl.DeviceIdType.MESH
F32 = jnp.float32
BF16 = jnp.bfloat16

Z, YL, X, YH, CORE = 8, 4, 4, 2, 2
ROWS, COLS = Z * YL, X * YH * CORE
TILE = 128
NODE = 256
WIDTH = 128
HID = 256
SLOTS = 128
ROW_TILES = COLS * NODE // TILE
COL_TILES = ROWS * NODE // TILE
SPLIT = 144
REST = NODE - SPLIT
VMEM_LIMIT = 56 * 1024 * 1024


def row_of(z, y):
    return z * YL + y


def col_of(x, yh, core):
    return (x * YH + yh) * CORE + core


def where_am_i():
    row = lax.axis_index("row")
    col = lax.axis_index("col")
    return row, col, row // YL, row % YL, col // (YH * CORE), (col // CORE) % YH, col % CORE


def greet(peers):
    barrier = pltpu.get_barrier_semaphore()
    for peer in peers:
        pl.semaphore_signal(barrier, inc=1, device_id=peer, device_id_type=MESH)


def greeted(count):
    pl.semaphore_wait(pltpu.get_barrier_semaphore(), count)


class Sender:
    def __init__(self, sems):
        self.sems = sems
        self.started = []
        self.waited = 0

    def send(self, src, dst, recv_sem, peer):
        copy = pltpu.make_async_remote_copy(
            src_ref=src,
            dst_ref=dst,
            send_sem=self.sems.at[len(self.started)],
            recv_sem=recv_sem,
            device_id=peer,
            device_id_type=MESH,
        )
        copy.start()
        self.started.append(copy)

    def finish(self, upto=None):
        for copy in self.started[self.waited:upto]:
            copy.wait_send()
        self.waited = len(self.started) if upto is None else upto


def arrived(dst, recv_sem, peer):
    pltpu.make_async_remote_copy(
        src_ref=dst, dst_ref=dst, send_sem=recv_sem, recv_sem=recv_sem, device_id=peer, device_id_type=MESH
    ).wait_recv()


HALF_Z = Z // 2
PIECES = 16
PIECE = WIDTH // PIECES
EXTRA = 8
UNROLL = 32
GATHER_SENDS = 3 + 28 + 7 + 24
MIDDLE_SENDS = 8 + 6 + 1 + 1 + 6 + 8
PARAM_SENDS = 1 + 3 + 1 + 3 + 7 + 1 + 6 + 8
SCATTER_SENDS = 28 + 3
SENDS = GATHER_SENDS + MIDDLE_SENDS + PARAM_SENDS + SCATTER_SENDS


def dot(a, b, ca, cb):
    return lax.dot_general(a, b, (((ca,), (cb,)), ((), ())), preferred_element_type=F32)


def plan(segment, pick, live, last_tile):
    n = SLOTS
    lane = lax.broadcasted_iota(jnp.int32, (n, n), 1)
    sub = lax.broadcasted_iota(jnp.int32, (n, n), 0)
    seg = jnp.where(live, segment, last_tile)
    seg_l = jnp.broadcast_to(seg, (n, n))
    seg_s = seg_l.T
    key_l = seg_l * n + lane
    key_s = seg_s * n + sub
    rank = jnp.sum((key_s < key_l).astype(jnp.int32), axis=0, keepdims=True)
    rank_s = jnp.broadcast_to(rank, (n, n)).T
    hot = (rank_s == lane).astype(jnp.int32)
    pick_s = jnp.broadcast_to(pick, (n, n)).T
    order = jnp.sum(hot * sub, axis=0, keepdims=True)
    picked = jnp.sum(hot * pick_s, axis=0, keepdims=True)
    placed = jnp.sum(hot * seg_s, axis=0, keepdims=True)
    before = jnp.sum((rank_s == lane - 1).astype(jnp.int32) * seg_s, axis=0, keepdims=True)
    keep = jnp.where((placed == before) & (lane[0:1] > 0), 1.0, 0.0)
    upto = jnp.sum((seg_s <= lane).astype(jnp.int32), axis=0, keepdims=True)
    exact = jnp.sum((seg_s == lane).astype(jnp.int32), axis=0, keepdims=True)
    last = jnp.maximum(upto - 1, 0)
    has = jnp.where(exact > 0, 1.0, 0.0)
    return order, picked, last, keep, has


def products(base, ints, floats, values, panel, run, contract):
    def group(g, acc):
        for u in range(UNROLL):
            i = g * UNROLL + u
            slot, tile = ints[base, i], ints[base + 1, i]
            acc = acc * floats[base, i] + dot(values[slot], panel[tile], contract, 0)
            run[i] = acc.astype(BF16)
        return acc

    lax.fori_loop(0, SLOTS // UNROLL, group, jnp.zeros((TILE, WIDTH), F32))


def whole_kernel(
    feat, weight_hbm, bias_hbm, grad_hbm, values_hbm, rows_hbm, cols_hbm, count_ref,
    hidden, gw_out, gb_out, result,
    weight, bias, grad_out, rows_ref, cols_ref,
    values, panel, run, partial, paired, pair_in, x_in, y_out, y_in, block, back,
    a_out, a_in, near_out, near_in,
    core_piece, core_piece_in, x_piece, x_piece_in, far_piece, far_piece_in, near_piece, near_piece_in, z_piece, z_piece_in,
    ints_v, floats_v, ints, floats,
    sends, load_sem, values_sem, table_sem, recv_a, recv_b, pair_sem, x_sem, y_sem, gather_sem, a_sem, near_sem,
    core_psem, x_psem, far_psem, near_psem, z_psem, last_sem,
):
    row, col, z, y, x, yh, core = where_am_i()
    up = (row_of((z + 1) % Z, y), col)
    down = (row_of((z + Z - 1) % Z, y), col)
    near = [(row_of(z, (y + j) % YL), col) for j in range(1, YL)]
    along = [(row_of((z + d) % Z, y), col) for d in range(1, Z)]
    sibling = (row, col_of(x, yh, 1 - core))
    far = (row, col_of(x, 1 - yh, core))
    ring = [(row, col_of((x + d) % X, yh, core)) for d in range(1, X)]
    greet([far] + along + ring + near + [sibling])
    early = [
        pltpu.make_async_copy(rows_hbm, rows_ref, load_sem.at[0]),
        pltpu.make_async_copy(cols_hbm, cols_ref, load_sem.at[1]),
    ]
    late = [
        pltpu.make_async_copy(feat, panel.at[row], load_sem.at[2]),
        pltpu.make_async_copy(values_hbm, values, values_sem),
    ]
    dense = [
        pltpu.make_async_copy(weight_hbm, weight, load_sem.at[3]),
        pltpu.make_async_copy(bias_hbm, bias, load_sem.at[4]),
        pltpu.make_async_copy(grad_hbm, grad_out, load_sem.at[5]),
    ]
    for copy in early + late + dense:
        copy.start()
    greeted(len(along + near + ring) + 2)
    out = Sender(sends)

    part_a, part_b = pl.ds(0, SPLIT), pl.ds(SPLIT, REST)

    def shard(dz, j):
        return row_of((z + Z + dz) % Z, (y + j) % YL)

    def a(s):
        return panel.at[s, part_a], recv_a.at[s]

    def b(s):
        return panel.at[s, part_b], recv_b.at[s]

    def pass_on(src, s, way, peer):
        dst, sem = way(s)
        out.send(src, dst, sem, peer)

    mine = feat.at[part_a], feat.at[part_b]
    pass_on(mine[1], row, b, up)
    pass_on(mine[1], row, b, down)
    for j in range(1, YL):
        pass_on(mine[0], row, a, near[j - 1])
    pass_on(mine[0], row, a, up)
    pass_on(mine[0], row, a, down)
    for j in range(1, YL):
        pass_on(mine[1], row, b, near[j - 1])

    for copy in early:
        copy.wait()
    live = lax.broadcasted_iota(jnp.int32, (1, SLOTS), 1) < count_ref[...]
    ints_v[...] = jnp.zeros_like(ints_v)
    floats_v[...] = jnp.zeros_like(floats_v)
    for base, segment, pick, tiles in ((0, rows_ref, cols_ref, ROW_TILES), (3, cols_ref, rows_ref, COL_TILES)):
        order, picked, last, keep, has = plan(segment[...], pick[...], live, tiles)
        ints_v[base:base + 1] = order
        ints_v[base + 1:base + 2] = picked
        ints_v[base + 2:base + 3] = last
        floats_v[base:base + 1] = keep
        floats_v[base + 2:base + 3] = has
    table = [
        pltpu.make_async_copy(ints_v, ints, table_sem.at[0]),
        pltpu.make_async_copy(floats_v, floats, table_sem.at[1]),
    ]
    for copy in table:
        copy.start()

    for j in range(1, YL):
        s = shard(0, j)
        arrived(*a(s), near[j - 1])
        pass_on(a(s)[0], s, a, up)
        pass_on(a(s)[0], s, a, down)
    for d in range(1, HALF_Z):
        for sign, source, target in ((-1, down, up), (1, up, down)):
            s = shard(sign * d, 0)
            arrived(*b(s), source)
            if d < HALF_Z - 1 or sign < 0:
                pass_on(b(s)[0], s, b, target)
            for j in range(1, YL):
                pass_on(b(s)[0], s, b, near[j - 1])
        for j in range(YL):
            for sign, source, target in ((-1, down, up), (1, up, down)):
                s = shard(sign * d, j)
                arrived(*a(s), source)
                if d < HALF_Z - 1 or (j < 2) == (sign < 0):
                    pass_on(a(s)[0], s, a, target)
    s = shard(HALF_Z, 0)
    arrived(*b(s), down)
    for j in range(1, YL):
        pass_on(b(s)[0], s, b, near[j - 1])
    for copy in table:
        copy.wait()
    for copy in late:
        copy.wait()
    for j in range(YL):
        arrived(*a(shard(HALF_Z, j)), down if j < 2 else up)
    for dz in range(Z):
        for j in range(1, YL):
            arrived(*b(shard(dz, j)), near[j - 1])

    products(0, ints, floats, values, panel.reshape(COL_TILES, TILE, WIDTH), run, 1)
    tiles_per = NODE // TILE
    gathered = len(out.started)
    order = [2, 1, 3, 0]

    def result_tile(base, r):
        return (run[ints[base, r]].astype(F32) * floats[base, r]).astype(BF16)

    for c in (1 - core, core):
        for h in range(YH):
            hh = (1 - yh) if h == 0 else yh
            for d in order:
                other = (x + d) % X
                for t in range(tiles_per):
                    partial[other, hh, c, t * TILE:(t + 1) * TILE] = result_tile(2, col_of(other, hh, c) * tiles_per + t)
                if c is not core:
                    out.send(partial.at[other, hh, c], pair_in.at[h, d], pair_sem.at[h, d], sibling)
    for h in range(YH):
        hh = (1 - yh) if h == 0 else yh
        for d in order:
            other = (x + d) % X
            arrived(pair_in.at[h, d], pair_sem.at[h, d], sibling)
            paired[h, d] = (partial[other, hh, core].astype(F32) + pair_in[h, d].astype(F32)).astype(BF16)
            if d:
                out.send(paired.at[h, d], x_in.at[h, X - d], x_sem.at[h, X - d], ring[d - 1])

    def summed(h):
        acc = paired[h, 0].astype(F32)
        for d in range(1, X):
            arrived(x_in.at[h, d], x_sem.at[h, d], ring[d - 1])
            acc += x_in[h, d].astype(F32)
        return acc

    out.finish(gathered)
    y_out[...] = summed(0).astype(BF16)
    out.send(y_out, y_in, y_sem.at[0], far)
    own = summed(1)
    arrived(y_in, y_sem.at[0], far)
    aggregate = (own + y_in[...].astype(F32)).astype(BF16)

    for copy in dense:
        copy.wait()
    preact = jnp.dot(aggregate, weight[...], preferred_element_type=F32) + bias[...]
    sigmoid = jax.nn.sigmoid(preact)
    slope = sigmoid * (1.0 + preact * (1.0 - sigmoid))
    grad_pre = (grad_out[...].astype(F32) * slope).astype(BF16)
    block[col] = dot(grad_pre, weight[...], 1, 1).astype(BF16)

    def g(c):
        return block.at[c], gather_sem.at[c]

    def share(c, peer):
        out.send(block.at[c], block.at[c], gather_sem.at[c], peer)

    share(col, far)
    for d in order[:3]:
        share(col, ring[d - 1])
    share(col, sibling)
    hidden[...] = (preact * sigmoid).astype(BF16)
    gw = dot(aggregate, grad_pre, 0, 0)
    gb = jnp.broadcast_to(jnp.sum(grad_pre.astype(F32), axis=0, keepdims=True), (EXTRA, HID))
    half = WIDTH // CORE
    for c in range(CORE):
        core_piece[c, :half] = gw[c * half:(c + 1) * half]
        core_piece[c, half:] = gb
    out.send(core_piece.at[1 - core], core_piece_in, core_psem.at[0], sibling)
    out.finish(len(out.started) - 6)
    arrived(core_piece_in, core_psem.at[0], sibling)
    quarter = half // X
    for q in range(X):
        for here, size, at in ((q * quarter, quarter, 0), (half, EXTRA, quarter)):
            x_piece[q, at:at + size] = core_piece[core, here:here + size] + core_piece_in[here:here + size]
    for d in range(1, X):
        out.send(x_piece.at[(x + d) % X], x_piece_in.at[X - d], x_psem.at[X - d], ring[d - 1])

    def from_ring(d, h):
        c = col_of((x + d) % X, h, core)
        arrived(*g(c), ring[d - 1])
        share(c, sibling)

    from_ring(1, yh)
    from_ring(3, yh)
    c = col_of(x, 1 - yh, core)
    arrived(*g(c), far)
    for d in order[:3]:
        share(c, ring[d - 1])
    share(c, sibling)
    from_ring(2, yh)
    acc = x_piece[x]
    for d in range(1, X):
        arrived(x_piece_in.at[d], x_psem.at[d], ring[d - 1])
        acc = acc + x_piece_in[d]
    z_piece[...] = acc
    for d in range(1, Z):
        out.send(z_piece, z_piece_in.at[Z - d], z_psem.at[Z - d], along[d - 1])
    for d in (1, 3, 2):
        from_ring(d, 1 - yh)
    for d in range(X):
        for h in range(YH):
            arrived(*g(col_of((x + d) % X, h, 1 - core)), sibling)

    products(3, ints, floats, values, block.reshape(ROW_TILES, TILE, WIDTH), run, 0)
    gathered = len(out.started)

    ways = ((0, 1, up, down), (1, -1, down, up))
    turns = (1, 2, 3, 0)

    def own_a(dz, j):
        return back.at[(z + Z + dz) % Z, (y + j) % YL]

    def build(dz, j):
        zz, yy = (z + Z + dz) % Z, (y + j) % YL
        for t in range(tiles_per):
            back[zz, yy, t * TILE:(t + 1) * TILE] = result_tile(5, row_of(zz, yy) * tiles_per + t)

    def begin(step, j, way, sign, target, source):
        build(sign * (HALF_Z - step), j)
        out.send(own_a(sign * (HALF_Z - step), j), a_in.at[way, step, j], a_sem.at[way, step, j], target)

    for j in (1, 2):
        begin(0, j, *(ways[0] if j < 2 else ways[1]))
    for j in (3, 0):
        begin(0, j, *(ways[0] if j < 2 else ways[1]))
    for j in turns:
        begin(1, j, *(ways[1] if j < 2 else ways[0]))
    for j in turns:
        build(HALF_Z - 1 if j < 2 else 1 - HALF_Z, j)
    acc = z_piece[...]
    for d in range(1, Z):
        arrived(z_piece_in.at[d], z_psem.at[d], along[d - 1])
        acc = acc + z_piece_in[d]
    for h in range(YH):
        far_piece[h, :PIECE] = acc[h * PIECE:(h + 1) * PIECE]
        far_piece[h, PIECE:] = acc[quarter:]
    out.send(far_piece.at[1 - yh], far_piece_in, far_psem.at[0], far)
    for dz in (2, -2):
        for j in turns:
            build(dz, j)

    def hop(step, j, way, sign, target, source):
        arrived(a_in.at[way, step - 1, j], a_sem.at[way, step - 1, j], source)
        a_out[way, step, j] = (
            own_a(sign * (HALF_Z - step), j)[...].astype(F32) + a_in[way, step - 1, j].astype(F32)
        ).astype(BF16)
        out.send(a_out.at[way, step, j], a_in.at[way, step, j], a_sem.at[way, step, j], target)

    for j in turns:
        hop(1, j, *(ways[0] if j < 2 else ways[1]))
    for dz in (1, -1, 0):
        for j in turns:
            build(dz, j)
    out.finish(gathered)
    arrived(far_piece_in, far_psem.at[0], far)
    near_piece[...] = far_piece[yh] + far_piece_in[...]
    for j in range(1, YL):
        out.send(near_piece, near_piece_in.at[YL - j], near_psem.at[YL - j], near[j - 1])
    for j in turns:
        for way in ways:
            hop(2, j, *way)
    acc = near_piece[...]
    for j in range(1, YL):
        arrived(near_piece_in.at[j], near_psem.at[j], near[j - 1])
        acc = acc + near_piece_in[j]

    def spot(x_at, h, c):
        return (c * X + x_at) * YH + h

    def last(p):
        return gw_out.at[p], last_sem.at[p]

    def spread(p, peer):
        out.send(gw_out.at[p], gw_out.at[p], last_sem.at[p], peer)

    gw_out[spot(x, yh, core)] = acc[:PIECE]
    gb_out[...] = acc[PIECE:]
    spread(spot(x, yh, core), far)
    for d in range(1, X):
        spread(spot(x, yh, core), ring[d - 1])
    spread(spot(x, yh, core), sibling)
    for j in turns:
        for way in ways:
            hop(3, j, *way)
    out.finish(len(out.started) - 16)
    p = spot(x, 1 - yh, core)
    arrived(*last(p), far)
    for d in range(1, X):
        spread(p, ring[d - 1])
    spread(p, sibling)

    def final_a(j):
        acc = own_a(0, j)[...].astype(F32)
        for way, _, _, source in ways:
            arrived(a_in.at[way, 3, j], a_sem.at[way, 3, j], source)
            acc += a_in[way, 3, j].astype(F32)
        return acc

    for j in range(1, YL):
        near_out[j] = final_a(j).astype(BF16)
        out.send(near_out.at[j], near_in.at[YL - j], near_sem.at[YL - j], near[j - 1])
    for d in range(1, X):
        for h in (yh, 1 - yh):
            p = spot((x + d) % X, h, core)
            arrived(*last(p), ring[d - 1])
            spread(p, sibling)
    total = final_a(0)
    for j in range(1, YL):
        arrived(near_in.at[j], near_sem.at[j], near[j - 1])
        total += near_in[j].astype(F32)
    result[...] = total.astype(BF16)
    for d in range(X):
        for h in range(YH):
            arrived(*last(spot((x + d) % X, h, 1 - core)), sibling)
    out.finish()


def whole(features, weight, bias, grad_out, values, rows, cols, count):
    vmem = pl.BlockSpec(memory_space=pltpu.VMEM)
    dma = pltpu.SemaphoreType.DMA
    return pl.pallas_call(
        whole_kernel,
        out_shape=(
            jax.ShapeDtypeStruct((NODE, HID), BF16),
            jax.ShapeDtypeStruct((PIECES, PIECE, HID), F32),
            jax.ShapeDtypeStruct((EXTRA, HID), F32),
            jax.ShapeDtypeStruct((NODE, WIDTH), BF16),
        ),
        in_specs=[pl.BlockSpec(memory_space=pl.ANY)] * 7 + [vmem],
        out_specs=(vmem,) * 4,
        scratch_shapes=[
            pltpu.VMEM((WIDTH, HID), BF16),
            pltpu.VMEM((1, HID), F32),
            pltpu.VMEM((NODE, HID), BF16),
            pltpu.VMEM((1, SLOTS), jnp.int32),
            pltpu.VMEM((1, SLOTS), jnp.int32),
            pltpu.VMEM((SLOTS, TILE, TILE), BF16),
            pltpu.VMEM((ROWS, NODE, WIDTH), BF16),
            pltpu.VMEM((SLOTS, TILE, WIDTH), BF16),
            pltpu.VMEM((X, YH, CORE, NODE, WIDTH), BF16),
            pltpu.VMEM((YH, X, NODE, WIDTH), BF16),
            pltpu.VMEM((YH, X, NODE, WIDTH), BF16),
            pltpu.VMEM((YH, X, NODE, WIDTH), BF16),
            pltpu.VMEM((NODE, WIDTH), BF16),
            pltpu.VMEM((NODE, WIDTH), BF16),
            pltpu.VMEM((COLS, NODE, WIDTH), BF16),
            pltpu.VMEM((Z, YL, NODE, WIDTH), BF16),
            pltpu.VMEM((2, 4, YL, NODE, WIDTH), BF16),
            pltpu.VMEM((2, 4, YL, NODE, WIDTH), BF16),
            pltpu.VMEM((YL, NODE, WIDTH), BF16),
            pltpu.VMEM((YL, NODE, WIDTH), BF16),
            pltpu.VMEM((CORE, WIDTH // CORE + EXTRA, HID), F32),
            pltpu.VMEM((WIDTH // CORE + EXTRA, HID), F32),
            pltpu.VMEM((X, WIDTH // CORE // X + EXTRA, HID), F32),
            pltpu.VMEM((X, WIDTH // CORE // X + EXTRA, HID), F32),
            pltpu.VMEM((YH, PIECE + EXTRA, HID), F32),
            pltpu.VMEM((PIECE + EXTRA, HID), F32),
            pltpu.VMEM((PIECE + EXTRA, HID), F32),
            pltpu.VMEM((YL, PIECE + EXTRA, HID), F32),
            pltpu.VMEM((WIDTH // CORE // X + EXTRA, HID), F32),
            pltpu.VMEM((Z, WIDTH // CORE // X + EXTRA, HID), F32),
            pltpu.VMEM((8, SLOTS), jnp.int32),
            pltpu.VMEM((8, SLOTS), F32),
            pltpu.SMEM((8, SLOTS), jnp.int32),
            pltpu.SMEM((8, SLOTS), F32),
            dma((SENDS,)),
            dma((6,)),
            dma,
            dma((2,)),
            dma((ROWS,)),
            dma((ROWS,)),
            dma((YH, X)),
            dma((YH, X)),
            dma((1,)),
            dma((COLS,)),
            dma((2, 4, YL)),
            dma((YL,)),
            dma((1,)),
            dma((X,)),
            dma((1,)),
            dma((YL,)),
            dma((Z,)),
            dma((PIECES,)),
        ],
        compiler_params=pltpu.CompilerParams(
            collective_id=0, has_side_effects=True, vmem_limit_bytes=VMEM_LIMIT
        ),
    )(features, weight, bias, grad_out, values, rows, cols, count)


def finish_kernel(hidden, gw, gb, result, hidden_out, gw_out, gb_out, result_out):
    hidden_out[...] = hidden[...]
    gw_out[...] = gw[...]
    gb_out[...] = gb[0:1]
    result_out[...] = result[...]


def finish(hidden, gw, gb, result):
    vmem = pl.BlockSpec(memory_space=pltpu.VMEM)
    return pl.pallas_call(
        finish_kernel,
        out_shape=(
            jax.ShapeDtypeStruct((NODE, HID), BF16),
            jax.ShapeDtypeStruct((WIDTH, HID), F32),
            jax.ShapeDtypeStruct((1, HID), F32),
            jax.ShapeDtypeStruct((NODE, WIDTH), BF16),
        ),
        in_specs=[vmem] * 4,
        out_specs=(vmem,) * 4,
    )(hidden, gw, gb, result)


def split_rows(outs):
    hidden, gw, gb, result = outs
    return hidden, gw.reshape(WIDTH, HID), gb, result


def per_device(features, weight, bias, grad_out, tile_values, tile_rows, tile_cols, tile_count):
    hidden, grad_weight, grad_bias, grad_features = finish(*split_rows(whole(
        features, weight, bias.reshape(1, HID), grad_out, tile_values[0, 0], tile_rows[0], tile_cols[0], tile_count
    )))
    return hidden, grad_weight, grad_bias[0], grad_features


def solution(mesh):
    return jax.shard_map(
        per_device,
        mesh=mesh,
        in_specs=(
            P(("col", "row"), None),
            P(),
            P(),
            P(("row", "col"), None),
            P("row", "col", None, None, None),
            P("row", "col", None),
            P("row", "col", None),
            P("row", "col"),
        ),
        out_specs=(P(("row", "col"), None), P(), P(), P(("col", "row"), None)),
        check_vma=False,
    )
```

```python
import functools

import jax
import jax.numpy as jnp
from jax import lax
from jax.experimental import pallas as pl
from jax.experimental.pallas import tpu as pltpu
from jax.sharding import PartitionSpec as P

MESH = pl.DeviceIdType.MESH
F32 = jnp.float32
BF16 = jnp.bfloat16

Z, YL, X, YH, CORE = 8, 4, 4, 2, 2
ROWS, COLS = Z * YL, X * YH * CORE
TILE = 128
NODE = 256
WIDTH = 128
HID = 256
SLOTS = 128
ROW_TILES = COLS * NODE // TILE
COL_TILES = ROWS * NODE // TILE
SPLIT = 144
REST = NODE - SPLIT
VMEM_LIMIT = 56 * 1024 * 1024


def row_of(z, y):
    return z * YL + y


def col_of(x, yh, core):
    return (x * YH + yh) * CORE + core


def where_am_i():
    row = lax.axis_index("row")
    col = lax.axis_index("col")
    return row, col, row // YL, row % YL, col // (YH * CORE), (col // CORE) % YH, col % CORE


def greet(peers):
    barrier = pltpu.get_barrier_semaphore()
    for peer in peers:
        pl.semaphore_signal(barrier, inc=1, device_id=peer, device_id_type=MESH)


def greeted(count):
    pl.semaphore_wait(pltpu.get_barrier_semaphore(), count)


class Sender:
    def __init__(self, sems):
        self.sems = sems
        self.started = []
        self.waited = 0

    def send(self, src, dst, recv_sem, peer):
        copy = pltpu.make_async_remote_copy(
            src_ref=src,
            dst_ref=dst,
            send_sem=self.sems.at[len(self.started)],
            recv_sem=recv_sem,
            device_id=peer,
            device_id_type=MESH,
        )
        copy.start()
        self.started.append(copy)

    def finish(self, upto=None):
        for copy in self.started[self.waited:upto]:
            copy.wait_send()
        self.waited = len(self.started) if upto is None else upto


def arrived(dst, recv_sem, peer):
    pltpu.make_async_remote_copy(
        src_ref=dst, dst_ref=dst, send_sem=recv_sem, recv_sem=recv_sem, device_id=peer, device_id_type=MESH
    ).wait_recv()


HALF_Z = Z // 2
PIECES = 16
PIECE = WIDTH // PIECES
EXTRA = 8
UNROLL = 32
GATHER_SENDS = 3 + 28 + 7 + 24
MIDDLE_SENDS = 8 + 6 + 1 + 1 + 6 + 8
PARAM_SENDS = 1 + 3 + 1 + 3 + 7 + 1 + 6 + 8
SCATTER_SENDS = 28 + 3
SENDS = GATHER_SENDS + MIDDLE_SENDS + PARAM_SENDS + SCATTER_SENDS


def dot(a, b, ca, cb):
    return lax.dot_general(a, b, (((ca,), (cb,)), ((), ())), preferred_element_type=F32)


def plan(segment, pick, live, last_tile):
    n = SLOTS
    lane = lax.broadcasted_iota(jnp.int32, (n, n), 1)
    sub = lax.broadcasted_iota(jnp.int32, (n, n), 0)
    seg = jnp.where(live, segment, last_tile)
    seg_l = jnp.broadcast_to(seg, (n, n))
    seg_s = seg_l.T
    key_l = seg_l * n + lane
    key_s = seg_s * n + sub
    rank = jnp.sum((key_s < key_l).astype(jnp.int32), axis=0, keepdims=True)
    rank_s = jnp.broadcast_to(rank, (n, n)).T
    hot = (rank_s == lane).astype(jnp.int32)
    pick_s = jnp.broadcast_to(pick, (n, n)).T
    order = jnp.sum(hot * sub, axis=0, keepdims=True)
    picked = jnp.sum(hot * pick_s, axis=0, keepdims=True)
    placed = jnp.sum(hot * seg_s, axis=0, keepdims=True)
    before = jnp.sum((rank_s == lane - 1).astype(jnp.int32) * seg_s, axis=0, keepdims=True)
    keep = jnp.where((placed == before) & (lane[0:1] > 0), 1.0, 0.0)
    upto = jnp.sum((seg_s <= lane).astype(jnp.int32), axis=0, keepdims=True)
    exact = jnp.sum((seg_s == lane).astype(jnp.int32), axis=0, keepdims=True)
    last = jnp.maximum(upto - 1, 0)
    has = jnp.where(exact > 0, 1.0, 0.0)
    return order, picked, last, keep, has


def products(base, ints, floats, values, panel, run, contract):
    def group(g, acc):
        for u in range(UNROLL):
            i = g * UNROLL + u
            slot, tile = ints[base, i], ints[base + 1, i]
            acc = acc * floats[base, i] + dot(values[slot], panel[tile], contract, 0)
            run[i] = acc.astype(BF16)
        return acc

    lax.fori_loop(0, SLOTS // UNROLL, group, jnp.zeros((TILE, WIDTH), F32))


def whole_kernel(
    feat, weight_hbm, bias_hbm, grad_hbm, values_hbm, rows_hbm, cols_hbm, count_ref,
    hidden, gw_out, gb_out, result,
    weight, bias, grad_out, rows_ref, cols_ref,
    values, panel, run, partial, paired, pair_in, x_in, y_out, y_in, block, back,
    a_out, a_in, near_out, near_in,
    core_piece, core_piece_in, x_piece, x_piece_in, far_piece, far_piece_in, near_piece, near_piece_in, z_piece, z_piece_in,
    ints_v, floats_v, ints, floats,
    sends, load_sem, values_sem, table_sem, recv_a, recv_b, pair_sem, x_sem, y_sem, gather_sem, a_sem, near_sem,
    core_psem, x_psem, far_psem, near_psem, z_psem, last_sem,
):
    row, col, z, y, x, yh, core = where_am_i()
    up = (row_of((z + 1) % Z, y), col)
    down = (row_of((z + Z - 1) % Z, y), col)
    near = [(row_of(z, (y + j) % YL), col) for j in range(1, YL)]
    along = [(row_of((z + d) % Z, y), col) for d in range(1, Z)]
    sibling = (row, col_of(x, yh, 1 - core))
    far = (row, col_of(x, 1 - yh, core))
    ring = [(row, col_of((x + d) % X, yh, core)) for d in range(1, X)]
    greet([far] + along + ring + near + [sibling])
    early = [
        pltpu.make_async_copy(rows_hbm, rows_ref, load_sem.at[0]),
        pltpu.make_async_copy(cols_hbm, cols_ref, load_sem.at[1]),
    ]
    late = [
        pltpu.make_async_copy(feat, panel.at[row], load_sem.at[2]),
        pltpu.make_async_copy(values_hbm, values, values_sem),
    ]
    dense = [
        pltpu.make_async_copy(weight_hbm, weight, load_sem.at[3]),
        pltpu.make_async_copy(bias_hbm, bias, load_sem.at[4]),
        pltpu.make_async_copy(grad_hbm, grad_out, load_sem.at[5]),
    ]
    for copy in early + late + dense:
        copy.start()
    greeted(len(along + near + ring) + 2)
    out = Sender(sends)

    part_a, part_b = pl.ds(0, SPLIT), pl.ds(SPLIT, REST)

    def shard(dz, j):
        return row_of((z + Z + dz) % Z, (y + j) % YL)

    def a(s):
        return panel.at[s, part_a], recv_a.at[s]

    def b(s):
        return panel.at[s, part_b], recv_b.at[s]

    def pass_on(src, s, way, peer):
        dst, sem = way(s)
        out.send(src, dst, sem, peer)

    mine = feat.at[part_a], feat.at[part_b]
    pass_on(mine[1], row, b, up)
    pass_on(mine[1], row, b, down)
    for j in range(1, YL):
        pass_on(mine[0], row, a, near[j - 1])
    pass_on(mine[0], row, a, up)
    pass_on(mine[0], row, a, down)
    for j in range(1, YL):
        pass_on(mine[1], row, b, near[j - 1])

    for copy in early:
        copy.wait()
    live = lax.broadcasted_iota(jnp.int32, (1, SLOTS), 1) < count_ref[...]
    ints_v[...] = jnp.zeros_like(ints_v)
    floats_v[...] = jnp.zeros_like(floats_v)
    for base, segment, pick, tiles in ((0, rows_ref, cols_ref, ROW_TILES), (3, cols_ref, rows_ref, COL_TILES)):
        order, picked, last, keep, has = plan(segment[...], pick[...], live, tiles)
        ints_v[base:base + 1] = order
        ints_v[base + 1:base + 2] = picked
        ints_v[base + 2:base + 3] = last
        floats_v[base:base + 1] = keep
        floats_v[base + 2:base + 3] = has
    table = [
        pltpu.make_async_copy(ints_v, ints, table_sem.at[0]),
        pltpu.make_async_copy(floats_v, floats, table_sem.at[1]),
    ]
    for copy in table:
        copy.start()

    for j in range(1, YL):
        s = shard(0, j)
        arrived(*a(s), near[j - 1])
        pass_on(a(s)[0], s, a, up)
        pass_on(a(s)[0], s, a, down)
    for d in range(1, HALF_Z):
        for sign, source, target in ((-1, down, up), (1, up, down)):
            s = shard(sign * d, 0)
            arrived(*b(s), source)
            if d < HALF_Z - 1 or sign < 0:
                pass_on(b(s)[0], s, b, target)
            for j in range(1, YL):
                pass_on(b(s)[0], s, b, near[j - 1])
        for j in range(YL):
            for sign, source, target in ((-1, down, up), (1, up, down)):
                s = shard(sign * d, j)
                arrived(*a(s), source)
                if d < HALF_Z - 1 or (j < 2) == (sign < 0):
                    pass_on(a(s)[0], s, a, target)
    s = shard(HALF_Z, 0)
    arrived(*b(s), down)
    for j in range(1, YL):
        pass_on(b(s)[0], s, b, near[j - 1])
    for copy in table:
        copy.wait()
    for copy in late:
        copy.wait()
    for j in range(YL):
        arrived(*a(shard(HALF_Z, j)), down if j < 2 else up)
    for dz in range(Z):
        for j in range(1, YL):
            arrived(*b(shard(dz, j)), near[j - 1])

    products(0, ints, floats, values, panel.reshape(COL_TILES, TILE, WIDTH), run, 1)
    tiles_per = NODE // TILE
    gathered = len(out.started)
    order = [2, 1, 3, 0]

    def result_tile(base, r):
        return (run[ints[base, r]].astype(F32) * floats[base, r]).astype(BF16)

    for c in (1 - core, core):
        for h in range(YH):
            hh = (1 - yh) if h == 0 else yh
            for d in order:
                other = (x + d) % X
                for t in range(tiles_per):
                    partial[other, hh, c, t * TILE:(t + 1) * TILE] = result_tile(2, col_of(other, hh, c) * tiles_per + t)
                if c is not core:
                    out.send(partial.at[other, hh, c], pair_in.at[h, d], pair_sem.at[h, d], sibling)
    for h in range(YH):
        hh = (1 - yh) if h == 0 else yh
        for d in order:
            other = (x + d) % X
            arrived(pair_in.at[h, d], pair_sem.at[h, d], sibling)
            paired[h, d] = (partial[other, hh, core].astype(F32) + pair_in[h, d].astype(F32)).astype(BF16)
            if d:
                out.send(paired.at[h, d], x_in.at[h, X - d], x_sem.at[h, X - d], ring[d - 1])

    def summed(h):
        acc = paired[h, 0].astype(F32)
        for d in range(1, X):
            arrived(x_in.at[h, d], x_sem.at[h, d], ring[d - 1])
            acc += x_in[h, d].astype(F32)
        return acc

    out.finish(gathered)
    y_out[...] = summed(0).astype(BF16)
    out.send(y_out, y_in, y_sem.at[0], far)
    own = summed(1)
    arrived(y_in, y_sem.at[0], far)
    aggregate = (own + y_in[...].astype(F32)).astype(BF16)

    for copy in dense:
        copy.wait()
    preact = jnp.dot(aggregate, weight[...], preferred_element_type=F32) + bias[...]
    sigmoid = jax.nn.sigmoid(preact)
    slope = sigmoid * (1.0 + preact * (1.0 - sigmoid))
    grad_pre = (grad_out[...].astype(F32) * slope).astype(BF16)
    block[col] = dot(grad_pre, weight[...], 1, 1).astype(BF16)

    def g(c):
        return block.at[c], gather_sem.at[c]

    def share(c, peer):
        out.send(block.at[c], block.at[c], gather_sem.at[c], peer)

    share(col, far)
    for d in order[:3]:
        share(col, ring[d - 1])
    share(col, sibling)
    hidden[...] = (preact * sigmoid).astype(BF16)
    gw = dot(aggregate, grad_pre, 0, 0)
    gb = jnp.broadcast_to(jnp.sum(grad_pre.astype(F32), axis=0, keepdims=True), (EXTRA, HID))
    half = WIDTH // CORE
    for c in range(CORE):
        core_piece[c, :half] = gw[c * half:(c + 1) * half]
        core_piece[c, half:] = gb
    out.send(core_piece.at[1 - core], core_piece_in, core_psem.at[0], sibling)
    out.finish(len(out.started) - 6)
    arrived(core_piece_in, core_psem.at[0], sibling)
    quarter = half // X
    for q in range(X):
        for here, size, at in ((q * quarter, quarter, 0), (half, EXTRA, quarter)):
            x_piece[q, at:at + size] = core_piece[core, here:here + size] + core_piece_in[here:here + size]
    for d in range(1, X):
        out.send(x_piece.at[(x + d) % X], x_piece_in.at[X - d], x_psem.at[X - d], ring[d - 1])

    def from_ring(d, h):
        c = col_of((x + d) % X, h, core)
        arrived(*g(c), ring[d - 1])
        share(c, sibling)

    from_ring(1, yh)
    from_ring(3, yh)
    c = col_of(x, 1 - yh, core)
    arrived(*g(c), far)
    for d in order[:3]:
        share(c, ring[d - 1])
    share(c, sibling)
    from_ring(2, yh)
    acc = x_piece[x]
    for d in range(1, X):
        arrived(x_piece_in.at[d], x_psem.at[d], ring[d - 1])
        acc = acc + x_piece_in[d]
    z_piece[...] = acc
    for d in range(1, Z):
        out.send(z_piece, z_piece_in.at[Z - d], z_psem.at[Z - d], along[d - 1])
    for d in (1, 3, 2):
        from_ring(d, 1 - yh)
    for d in range(X):
        for h in range(YH):
            arrived(*g(col_of((x + d) % X, h, 1 - core)), sibling)

    products(3, ints, floats, values, block.reshape(ROW_TILES, TILE, WIDTH), run, 0)
    gathered = len(out.started)

    ways = ((0, 1, up, down), (1, -1, down, up))
    turns = (1, 2, 3, 0)

    def own_a(dz, j):
        return back.at[(z + Z + dz) % Z, (y + j) % YL]

    def build(dz, j):
        zz, yy = (z + Z + dz) % Z, (y + j) % YL
        for t in range(tiles_per):
            back[zz, yy, t * TILE:(t + 1) * TILE] = result_tile(5, row_of(zz, yy) * tiles_per + t)

    def begin(step, j, way, sign, target, source):
        build(sign * (HALF_Z - step), j)
        out.send(own_a(sign * (HALF_Z - step), j), a_in.at[way, step, j], a_sem.at[way, step, j], target)

    for j in (1, 2):
        begin(0, j, *(ways[0] if j < 2 else ways[1]))
    for j in (3, 0):
        begin(0, j, *(ways[0] if j < 2 else ways[1]))
    for j in turns:
        begin(1, j, *(ways[1] if j < 2 else ways[0]))
    for j in turns:
        build(HALF_Z - 1 if j < 2 else 1 - HALF_Z, j)
    acc = z_piece[...]
    for d in range(1, Z):
        arrived(z_piece_in.at[d], z_psem.at[d], along[d - 1])
        acc = acc + z_piece_in[d]
    for h in range(YH):
        far_piece[h, :PIECE] = acc[h * PIECE:(h + 1) * PIECE]
        far_piece[h, PIECE:] = acc[quarter:]
    out.send(far_piece.at[1 - yh], far_piece_in, far_psem.at[0], far)
    for dz in (2, -2):
        for j in turns:
            build(dz, j)

    def hop(step, j, way, sign, target, source):
        arrived(a_in.at[way, step - 1, j], a_sem.at[way, step - 1, j], source)
        a_out[way, step, j] = (
            own_a(sign * (HALF_Z - step), j)[...].astype(F32) + a_in[way, step - 1, j].astype(F32)
        ).astype(BF16)
        out.send(a_out.at[way, step, j], a_in.at[way, step, j], a_sem.at[way, step, j], target)

    for j in turns:
        hop(1, j, *(ways[0] if j < 2 else ways[1]))
    for dz in (1, -1, 0):
        for j in turns:
            build(dz, j)
    out.finish(gathered)
    arrived(far_piece_in, far_psem.at[0], far)
    near_piece[...] = far_piece[yh] + far_piece_in[...]
    for j in range(1, YL):
        out.send(near_piece, near_piece_in.at[YL - j], near_psem.at[YL - j], near[j - 1])
    for j in turns:
        for way in ways:
            hop(2, j, *way)
    acc = near_piece[...]
    for j in range(1, YL):
        arrived(near_piece_in.at[j], near_psem.at[j], near[j - 1])
        acc = acc + near_piece_in[j]

    def spot(x_at, h, c):
        return (c * X + x_at) * YH + h

    def last(p):
        return gw_out.at[p], last_sem.at[p]

    def spread(p, peer):
        out.send(gw_out.at[p], gw_out.at[p], last_sem.at[p], peer)

    gw_out[spot(x, yh, core)] = acc[:PIECE]
    gb_out[...] = acc[PIECE:PIECE + 1]
    spread(spot(x, yh, core), far)
    for d in range(1, X):
        spread(spot(x, yh, core), ring[d - 1])
    spread(spot(x, yh, core), sibling)
    for j in turns:
        for way in ways:
            hop(3, j, *way)
    out.finish(len(out.started) - 16)
    p = spot(x, 1 - yh, core)
    arrived(*last(p), far)
    for d in range(1, X):
        spread(p, ring[d - 1])
    spread(p, sibling)

    def final_a(j):
        acc = own_a(0, j)[...].astype(F32)
        for way, _, _, source in ways:
            arrived(a_in.at[way, 3, j], a_sem.at[way, 3, j], source)
            acc += a_in[way, 3, j].astype(F32)
        return acc

    for j in range(1, YL):
        near_out[j] = final_a(j).astype(BF16)
        out.send(near_out.at[j], near_in.at[YL - j], near_sem.at[YL - j], near[j - 1])
    for d in range(1, X):
        for h in (yh, 1 - yh):
            p = spot((x + d) % X, h, core)
            arrived(*last(p), ring[d - 1])
            spread(p, sibling)
    total = final_a(0)
    for j in range(1, YL):
        arrived(near_in.at[j], near_sem.at[j], near[j - 1])
        total += near_in[j].astype(F32)
    result[...] = total.astype(BF16)
    for d in range(X):
        for h in range(YH):
            arrived(*last(spot((x + d) % X, h, 1 - core)), sibling)
    out.finish()


def whole(features, weight, bias, grad_out, values, rows, cols, count):
    vmem = pl.BlockSpec(memory_space=pltpu.VMEM)
    dma = pltpu.SemaphoreType.DMA
    return pl.pallas_call(
        whole_kernel,
        out_shape=(
            jax.ShapeDtypeStruct((NODE, HID), BF16),
            jax.ShapeDtypeStruct((PIECES, PIECE, HID), F32),
            jax.ShapeDtypeStruct((1, HID), F32),
            jax.ShapeDtypeStruct((NODE, WIDTH), BF16),
        ),
        in_specs=[pl.BlockSpec(memory_space=pl.ANY)] * 7 + [vmem],
        out_specs=(vmem,) * 4,
        scratch_shapes=[
            pltpu.VMEM((WIDTH, HID), BF16),
            pltpu.VMEM((1, HID), F32),
            pltpu.VMEM((NODE, HID), BF16),
            pltpu.VMEM((1, SLOTS), jnp.int32),
            pltpu.VMEM((1, SLOTS), jnp.int32),
            pltpu.VMEM((SLOTS, TILE, TILE), BF16),
            pltpu.VMEM((ROWS, NODE, WIDTH), BF16),
            pltpu.VMEM((SLOTS, TILE, WIDTH), BF16),
            pltpu.VMEM((X, YH, CORE, NODE, WIDTH), BF16),
            pltpu.VMEM((YH, X, NODE, WIDTH), BF16),
            pltpu.VMEM((YH, X, NODE, WIDTH), BF16),
            pltpu.VMEM((YH, X, NODE, WIDTH), BF16),
            pltpu.VMEM((NODE, WIDTH), BF16),
            pltpu.VMEM((NODE, WIDTH), BF16),
            pltpu.VMEM((COLS, NODE, WIDTH), BF16),
            pltpu.VMEM((Z, YL, NODE, WIDTH), BF16),
            pltpu.VMEM((2, 4, YL, NODE, WIDTH), BF16),
            pltpu.VMEM((2, 4, YL, NODE, WIDTH), BF16),
            pltpu.VMEM((YL, NODE, WIDTH), BF16),
            pltpu.VMEM((YL, NODE, WIDTH), BF16),
            pltpu.VMEM((CORE, WIDTH // CORE + EXTRA, HID), F32),
            pltpu.VMEM((WIDTH // CORE + EXTRA, HID), F32),
            pltpu.VMEM((X, WIDTH // CORE // X + EXTRA, HID), F32),
            pltpu.VMEM((X, WIDTH // CORE // X + EXTRA, HID), F32),
            pltpu.VMEM((YH, PIECE + EXTRA, HID), F32),
            pltpu.VMEM((PIECE + EXTRA, HID), F32),
            pltpu.VMEM((PIECE + EXTRA, HID), F32),
            pltpu.VMEM((YL, PIECE + EXTRA, HID), F32),
            pltpu.VMEM((WIDTH // CORE // X + EXTRA, HID), F32),
            pltpu.VMEM((Z, WIDTH // CORE // X + EXTRA, HID), F32),
            pltpu.VMEM((8, SLOTS), jnp.int32),
            pltpu.VMEM((8, SLOTS), F32),
            pltpu.SMEM((8, SLOTS), jnp.int32),
            pltpu.SMEM((8, SLOTS), F32),
            dma((SENDS,)),
            dma((6,)),
            dma,
            dma((2,)),
            dma((ROWS,)),
            dma((ROWS,)),
            dma((YH, X)),
            dma((YH, X)),
            dma((1,)),
            dma((COLS,)),
            dma((2, 4, YL)),
            dma((YL,)),
            dma((1,)),
            dma((X,)),
            dma((1,)),
            dma((YL,)),
            dma((Z,)),
            dma((PIECES,)),
        ],
        compiler_params=pltpu.CompilerParams(
            collective_id=0, has_side_effects=True, vmem_limit_bytes=VMEM_LIMIT
        ),
    )(features, weight, bias, grad_out, values, rows, cols, count)


def finish_kernel(*refs):
    half = len(refs) // 2
    copies = [pltpu.make_async_copy(refs[i], refs[half + i], refs[-1].at[i]) for i in range(half)]
    for copy in copies:
        copy.start()
    for copy in copies:
        copy.wait()


def finish(*arrays):
    anywhere = pl.BlockSpec(memory_space=pl.ANY)
    return pl.pallas_call(
        finish_kernel,
        out_shape=tuple(jax.ShapeDtypeStruct(a.shape, a.dtype) for a in arrays),
        in_specs=[anywhere] * len(arrays),
        out_specs=(anywhere,) * len(arrays),
        scratch_shapes=[pltpu.SemaphoreType.DMA((len(arrays),))],
    )(*arrays)


def split_rows(outs):
    hidden, gw, gb, result = outs
    return hidden, gw.reshape(WIDTH, HID), gb, result


def per_device(features, weight, bias, grad_out, tile_values, tile_rows, tile_cols, tile_count):
    hidden, grad_weight, grad_bias, grad_features = finish(*split_rows(whole(
        features, weight, bias.reshape(1, HID), grad_out, tile_values[0, 0], tile_rows[0], tile_cols[0], tile_count
    )))
    return hidden, grad_weight, grad_bias[0], grad_features


def solution(mesh):
    return jax.shard_map(
        per_device,
        mesh=mesh,
        in_specs=(
            P(("col", "row"), None),
            P(),
            P(),
            P(("row", "col"), None),
            P("row", "col", None, None, None),
            P("row", "col", None),
            P("row", "col", None),
            P("row", "col"),
        ),
        out_specs=(P(("row", "col"), None), P(), P(), P(("col", "row"), None)),
        check_vma=False,
    )
```
